32 devices in a mesh: groups: 2 (over x), wide: 16 (over z, y, core).
Axes of the slice: x: 2, y: 2, z: 4, core: 2. Of those that a mesh axis runs over, the one named last changes fastest.
Arguments:
- tile_values: bfloat16 [256, 512, 512], P(('groups', 'wide')), parts along dimension 0, may hold values from -1.5 to 1.5
- tile_cols: int32 [32, 8], P(('groups', 'wide')), parts along dimension 0, may hold values from 0 to 15, as said below
- tile_counts: int32 [32], P(('groups', 'wide')), parts along dimension 0, may hold values from 2 to 8, as said below
Outputs:
- product_band: bfloat16 [32, 10, 512, 512], P(('groups', 'wide')), parts along dimension 0
The draws below stay inside these ranges and needn't reach their ends.
There are 2 independent parts, one for each index of `groups`. The reference program is written for one: setup_inputs(seed, part) draws one part's arguments, and reference() takes and returns one part's arrays. A program takes and returns all parts, laid end to end along the dimension named above; each array names one. Nothing has to cross between parts.
Inputs may be any that keep to these rules, and one draw needn't show every extreme that they name: `tile_cols`: in every tile row i, slot 0 holds column i and slot 1 holds column (i + 1) mod 16; the columns of one row are distinct and lie within 4 tiles of i, counted around the loop of 16 tile columns. `tile_counts`: some tile row holds 8 tiles, some holds 2.
All inputs are finite; a program needn't handle non-finite values.
Results may differ from the reference program's by a relative error of at most 0.001.
Values may be sent and summed in bfloat16 or wider, within the bound.
No kernel may reach another device: no remote copies, remote signals or barrier semaphores. Data moves between devices by JAX's collectives and lax.ppermute only.
A program may use at most 128 MiB of HBM per device.

```python
import jax
import jax.numpy as jnp
from jax import lax

B = 512
W = 4
MAXT = 8
SLOTS = 128
N_WIDE = 16


def draw_tile_cols(key, part):
    key = jax.random.fold_in(key, 11)
    rows = jnp.arange(N_WIDE, dtype=jnp.int32)
    below = jnp.arange(-W, 0, dtype=jnp.int32)
    above = jnp.arange(2, W + 1, dtype=jnp.int32)
    candidates = jnp.concatenate([below, above])
    keys = jax.random.split(key, N_WIDE)
    picked = jax.vmap(lambda k: jax.random.permutation(k, candidates)[:MAXT - 2])(keys)
    fixed_offs = jnp.broadcast_to(jnp.array([0, 1], dtype=jnp.int32), (N_WIDE, 2))
    offsets = jnp.concatenate([fixed_offs, picked], axis=1)
    return ((rows[:, None] + offsets) % N_WIDE).astype(jnp.int32)


def draw_tile_counts(key, part):
    key = jax.random.fold_in(key, 23)
    first_key, second_key, third_key = jax.random.split(key, 3)
    counts = jax.random.randint(first_key, (N_WIDE,), 2, MAXT + 1, dtype=jnp.int32)
    top_rank = jax.random.randint(second_key, (), 0, N_WIDE, dtype=jnp.int32)
    step_away = jax.random.randint(third_key, (), 1, N_WIDE, dtype=jnp.int32)
    low_rank = (top_rank + step_away) % N_WIDE
    counts = counts.at[top_rank].set(MAXT)
    counts = counts.at[low_rank].set(2)
    return counts.astype(jnp.int32)


def shard_levels(key, shape, shards, smallest, high):
    def one(axis_at, blocks):
        steps = jax.random.uniform(jax.random.fold_in(jax.random.fold_in(key, 6), axis_at), (blocks,), jnp.float32, smallest / len(shards), high / len(shards))
        return jnp.repeat(jnp.exp(steps), shape[axis_at] // blocks).reshape((-1,) + (1,) * (len(shape) - axis_at - 1))

    gain = one(*shards[0])
    for cut in shards[1:]:
        gain = gain * one(*cut)
    return gain


def scatter_about(own_key, dims, spread, bound, cuts=(), held_as=jnp.bfloat16):
    entries = jax.random.normal(own_key, dims, jnp.float32) * spread
    if len(cuts) > 0:
        entries = shard_levels(own_key, dims, cuts, -0.22, 0.18) * entries
    return jnp.clip(entries, min=-bound, max=bound).astype(held_as)


def setup_inputs(seed: int = 0, part: int = 0) -> dict:
    arg_keys = jax.random.split(jax.random.key(seed), 4)
    own_keys = jax.random.split(jax.random.fold_in(arg_keys[3], part), 4)
    tile_values = scatter_about(own_keys[0], (SLOTS, B, B), 0.2102, 1.5, ((0, 16),))
    tile_cols = draw_tile_cols(jax.random.fold_in(jax.random.fold_in(arg_keys[3], part), 71), part)
    tile_counts = draw_tile_counts(jax.random.fold_in(jax.random.fold_in(arg_keys[3], part), 71), part)
    return {"tile_values": tile_values, "tile_cols": tile_cols, "tile_counts": tile_counts}


def reference(tile_values, tile_cols, tile_counts):
    vals = tile_values.reshape(N_WIDE, MAXT, B, B)
    live = jnp.arange(MAXT, dtype=jnp.int32)[None, :] < tile_counts[:, None]
    masked = jnp.where(live[:, :, None, None], vals, jnp.zeros((), vals.dtype))
    rows = jnp.arange(N_WIDE, dtype=jnp.int32)

    def one_row(here):
        after = (here + 1) % N_WIDE
        own = lax.dynamic_index_in_dim(masked, here, 0, keepdims=False).astype(jnp.float32)
        nxt = lax.dynamic_index_in_dim(masked, after, 0, keepdims=False).astype(jnp.float32)
        own_cols = lax.dynamic_index_in_dim(tile_cols, here, 0, keepdims=False)
        nxt_cols = lax.dynamic_index_in_dim(tile_cols, after, 0, keepdims=False)
        band = jnp.zeros((2 * W + 2, B, B), jnp.float32)
        first = jnp.einsum("ij,sjk->sik", own[0], own, precision=lax.Precision.HIGHEST)
        band = band.at[((own_cols - here + W) % N_WIDE).astype(jnp.int32)].add(first)
        second = jnp.einsum("ij,sjk->sik", own[1], nxt, precision=lax.Precision.HIGHEST)
        band = band.at[((nxt_cols - here + W) % N_WIDE).astype(jnp.int32)].add(second)
        return band.astype(jnp.bfloat16)

    return lax.map(one_row, rows)
```

```python
import functools

import jax
import jax.numpy as jnp
from jax import lax
from jax.experimental import pallas as pl
from jax.experimental.pallas import tpu as pltpu
from jax.sharding import PartitionSpec as P

W = 4
WIDTH = 2 * W + 2
CHUNKS = ((0, 1), (1, 4), (4, 7), (7, 8))
ANY = pl.BlockSpec(memory_space=pl.ANY)
SMEM = pl.BlockSpec(memory_space=pltpu.SMEM)


def find(cols_ref, counts_ref, col):
    found = jnp.int32(-1)
    for s in range(cols_ref.shape[1]):
        found = jnp.where((cols_ref[0, s] == col) & (s < counts_ref[0]), s, found)
    return found


def dot(a, b):
    return jnp.dot(a, b, preferred_element_type=jnp.float32)


def band_kernel(first_slot, jobs, total, *refs):
    cols, counts, next_cols, next_counts, own = refs[:5]
    chunk = refs[5] if first_slot >= 0 else None
    (out, own_v, recv_v, out_v, sem_fixed, sem_own, sem_recv, sem_out) = refs[-8:]
    here = cols[0, 0]

    def job(t):
        if first_slot >= 0:
            slot = first_slot + t
            col = next_cols[0, slot]
            active = slot < next_counts[0]
        else:
            col = lax.rem(here + t - W + total, total)
            active = find(next_cols, next_counts, col) < 0
        k = lax.rem(col - here + W + total, total)
        return active, k, find(cols, counts, col)

    def fixed(i):
        return pltpu.make_async_copy(own.at[i], own_v.at[i], sem_fixed.at[i])

    def own_copy(t, f):
        return pltpu.make_async_copy(own.at[f], own_v.at[2 + t], sem_own.at[t])

    def recv_copy(t):
        return pltpu.make_async_copy(chunk.at[t], recv_v.at[t], sem_recv.at[t])

    def out_copy(t, k):
        return pltpu.make_async_copy(out_v.at[t], out.at[0, k], sem_out.at[t])

    if first_slot >= 0:
        fixed(1).start()
    fixed(0).start()

    @pl.loop(0, jobs)
    def _(t):
        active, k, f = job(t)

        @pl.when(active)
        def _():
            if first_slot >= 0:
                recv_copy(t).start()

            @pl.when(f >= 0)
            def _():
                own_copy(t, f).start()

    if first_slot >= 0:
        fixed(1).wait()
    fixed(0).wait()

    @pl.loop(0, jobs)
    def _(t):
        active, k, f = job(t)

        @pl.when(active)
        def _():
            if first_slot >= 0:
                recv_copy(t).wait()

            @pl.when(f >= 0)
            def _():
                own_copy(t, f).wait()
                acc = dot(own_v[0], own_v[2 + t])
                if first_slot >= 0:
                    acc = acc + dot(own_v[1], recv_v[t])
                out_v[t] = acc.astype(out_v.dtype)

            @pl.when(f < 0)
            def _():
                if first_slot >= 0:
                    out_v[t] = dot(own_v[1], recv_v[t]).astype(out_v.dtype)
                else:
                    out_v[t] = jnp.zeros(out_v.shape[1:], out_v.dtype)

            out_copy(t, k).start()

    @pl.loop(0, jobs)
    def _(t):
        active, k, f = job(t)

        @pl.when(active)
        def _():
            out_copy(t, k).wait()


def band_call(first_slot, jobs, total, meta, own, chunk=None, band=None):
    b = own.shape[1:]
    operands = [*meta, own]
    specs = [SMEM] * 4 + [ANY]
    aliases = {}
    if chunk is not None:
        operands.append(chunk)
        specs.append(ANY)
    if band is not None:
        aliases = {len(operands): 0}
        operands.append(band)
        specs.append(ANY)
    tile_bytes = b[0] * b[1] * 2
    return pl.pallas_call(
        functools.partial(band_kernel, first_slot, jobs, total),
        out_shape=jax.ShapeDtypeStruct((1, WIDTH) + b, own.dtype),
        in_specs=specs,
        out_specs=ANY,
        input_output_aliases=aliases,
        scratch_shapes=[
            pltpu.VMEM((2 + jobs,) + b, own.dtype),
            pltpu.VMEM((jobs if chunk is not None else 1,) + b, own.dtype),
            pltpu.VMEM((jobs,) + b, own.dtype),
            pltpu.SemaphoreType.DMA((2,)),
            pltpu.SemaphoreType.DMA((jobs,)),
            pltpu.SemaphoreType.DMA((jobs,)),
            pltpu.SemaphoreType.DMA((jobs,)),
        ],
        compiler_params=pltpu.CompilerParams(vmem_limit_bytes=40 * 2**20),
        cost_estimate=pl.CostEstimate(
            flops=jobs * 4 * b[0] * b[0] * b[1],
            bytes_accessed=(3 * jobs + 2) * tile_bytes,
            transcendentals=0,
        ),
    )(*operands)


def per_device(tile_values, tile_cols, tile_counts):
    total = lax.axis_size("wide")
    pairs = [(i, (i - 1) % total) for i in range(total)]
    send = lambda value: lax.ppermute(value, "wide", pairs)
    chunks = [send(tile_values[a:b]) for a, b in CHUNKS]
    meta = (tile_cols, tile_counts, send(tile_cols), send(tile_counts))
    band = band_call(-1, WIDTH, total, meta, tile_values)
    for (a, b), chunk in zip(CHUNKS, chunks):
        band = band_call(a, b - a, total, meta, tile_values, chunk, band)
    return band


def solution(mesh):
    placed = (P(("groups", "wide"), None, None), P(("groups", "wide"), None), P(("groups", "wide")))
    return jax.shard_map(
        per_device,
        mesh=mesh,
        in_specs=placed,
        out_specs=P(("groups", "wide"), None, None, None),
        check_vma=False,
    )
```

```python
import functools

import jax
import jax.numpy as jnp
from jax import lax
from jax.experimental import pallas as pl
from jax.experimental.pallas import tpu as pltpu
from jax.sharding import PartitionSpec as P

W = 4
WIDTH = 2 * W + 2
META_ROWS = 16
HEAD = ((0, 1),)
LATER = ((1, 3), (3, 5), (5, 7), (7, 8))
ANY = pl.BlockSpec(memory_space=pl.ANY)
HBM = pl.BlockSpec(memory_space=pltpu.HBM)
SMEM = pl.BlockSpec(memory_space=pltpu.SMEM)
VMEM = pl.BlockSpec(memory_space=pltpu.VMEM)


def find(cols_ref, counts_ref, col):
    found = jnp.int32(-1)
    for s in range(cols_ref.shape[1]):
        found = jnp.where((cols_ref[0, s] == col) & (s < counts_ref[0]), s, found)
    return found


def dot(a, b):
    return jnp.dot(a, b, preferred_element_type=jnp.float32)


def finish(own, f, right, out_v, t):
    @pl.when(f >= 0)
    def _():
        acc = dot(own[0], own[f])
        if right is not None:
            acc = acc + dot(own[1], right())
        out_v[t] = acc.astype(out_v.dtype)

    @pl.when(f < 0)
    def _():
        if right is not None:
            out_v[t] = dot(own[1], right()).astype(out_v.dtype)
        else:
            out_v[t] = jnp.zeros(out_v.shape[1:], out_v.dtype)


def early_kernel(total, cols, counts, next_cols, next_counts, own, head, out, out_v, sems):
    here = cols[0, 0]

    def job(k):
        col = lax.rem(here + k - W + total, total)
        return find(cols, counts, col), find(next_cols, next_counts, col)

    def out_copy(k):
        return pltpu.make_async_copy(out_v.at[k], out.at[0, k], sems.at[k])

    @pl.loop(0, WIDTH)
    def _(k):
        f, s = job(k)

        @pl.when(s < 1)
        def _():
            @pl.when(s < 0)
            def _():
                finish(own, f, None, out_v, k)

            @pl.when(s == 0)
            def _():
                finish(own, f, lambda: head[: own.shape[1]], out_v, k)

            out_copy(k).start()

    @pl.loop(0, WIDTH)
    def _(k):
        _, s = job(k)

        @pl.when(s < 1)
        def _():
            out_copy(k).wait()


def chunk_kernel(first_slot, jobs, total, cols, counts, next_cols, next_counts, own, chunk, band, out, out_v, sems):
    here = cols[0, 0]
    rows = own.shape[1]

    def job(t):
        slot = first_slot + t
        col = next_cols[0, slot]
        return slot < next_counts[0], lax.rem(col - here + W + total, total), col

    def out_copy(t, k):
        return pltpu.make_async_copy(out_v.at[t], out.at[0, k], sems.at[t])

    @pl.loop(0, jobs)
    def _(t):
        active, k, col = job(t)

        @pl.when(active)
        def _():
            finish(own, find(cols, counts, col), lambda: chunk[pl.ds(pl.multiple_of(t * rows, rows), rows)], out_v, t)
            out_copy(t, k).start()

    @pl.loop(0, jobs)
    def _(t):
        active, k, _ = job(t)

        @pl.when(active)
        def _():
            out_copy(t, k).wait()


def call(kernel, jobs, operands, specs, aliases):
    own = operands[4]
    b = own.shape[1:]
    tile_bytes = b[0] * b[1] * 2
    return pl.pallas_call(
        kernel,
        out_shape=jax.ShapeDtypeStruct((1, WIDTH) + b, own.dtype),
        in_specs=specs,
        out_specs=ANY,
        input_output_aliases=aliases,
        scratch_shapes=[pltpu.VMEM((jobs,) + b, own.dtype), pltpu.SemaphoreType.DMA((jobs,))],
        compiler_params=pltpu.CompilerParams(vmem_limit_bytes=32 * 2**20),
        cost_estimate=pl.CostEstimate(
            flops=jobs * 4 * b[0] * b[0] * b[1],
            bytes_accessed=jobs * tile_bytes,
            transcendentals=0,
        ),
    )(*operands)


def pack_kernel(ranges, noted, *refs):
    cols, counts, own = refs[:3]
    parts, sems = refs[-1 - len(ranges) : -1], refs[-1]
    rows, lanes = own.shape[1:]
    copies = []
    for (a, b), part in zip(ranges, parts):
        for s in range(a, b):
            copies.append(pltpu.make_async_copy(own.at[s], part.at[pl.ds((s - a) * rows, rows)], sems.at[s]))
    for copy in copies:
        copy.start()
    if noted:
        lane = lax.broadcasted_iota(jnp.int32, (META_ROWS, lanes), 1)
        note = jnp.zeros((META_ROWS, lanes), jnp.int32)
        slots = cols.shape[1]
        for s in range(slots):
            note = jnp.where(lane == s, cols[0, s], note)
        note = jnp.where(lane == slots, counts[0], note)
        start = (ranges[0][1] - ranges[0][0]) * rows
        parts[0][pl.ds(start, META_ROWS)] = note.astype(jnp.float32).astype(parts[0].dtype)
    for copy in copies:
        copy.wait()


def pack(ranges, noted, cols, counts, own, *after):
    slots, rows, lanes = own.shape
    sizes = [(b - a) * rows for a, b in ranges]
    if noted:
        sizes[0] += META_ROWS
    return pl.pallas_call(
        functools.partial(pack_kernel, ranges, noted),
        out_shape=[jax.ShapeDtypeStruct((size, lanes), own.dtype) for size in sizes],
        in_specs=[SMEM] * 2 + [HBM] + [ANY] * len(after),
        out_specs=[VMEM] * len(sizes),
        scratch_shapes=[pltpu.SemaphoreType.DMA((slots,))],
        compiler_params=pltpu.CompilerParams(vmem_limit_bytes=32 * 2**20),
        cost_estimate=pl.CostEstimate(flops=0, bytes_accessed=8 * sum(sizes) * lanes, transcendentals=0),
    )(cols, counts, pltpu.with_memory_space_constraint(own, pltpu.HBM), *after)


def per_device(tile_values, tile_cols, tile_counts):
    total = lax.axis_size("wide")
    slots, rows, _ = tile_values.shape
    pairs = [(i, (i - 1) % total) for i in range(total)]
    send = lambda value: lax.ppermute(value, "wide", pairs)

    (first,) = pack(HEAD, True, tile_cols, tile_counts, tile_values)
    head = send(first)
    chunks = [send(part) for part in pack(LATER, False, tile_cols, tile_counts, tile_values, first)]

    got = head[rows, : slots + 1].astype(jnp.int32)
    meta = (tile_cols, tile_counts, got[None, :slots], got[slots:])
    band = call(
        functools.partial(early_kernel, total), WIDTH,
        (*meta, tile_values, head), [SMEM] * 4 + [VMEM] * 2, {},
    )
    for (a, b), chunk in zip(LATER, chunks):
        band = call(
            functools.partial(chunk_kernel, a, b - a, total), b - a,
            (*meta, tile_values, chunk, band), [SMEM] * 4 + [VMEM] * 2 + [ANY], {6: 0},
        )
    return band


def solution(mesh):
    placed = (P(("groups", "wide"), None, None), P(("groups", "wide"), None), P(("groups", "wide")))
    return jax.shard_map(
        per_device,
        mesh=mesh,
        in_specs=placed,
        out_specs=P(("groups", "wide"), None, None, None),
        check_vma=False,
    )
```

```python
import functools

import jax
import jax.numpy as jnp
from jax import lax
from jax.experimental import pallas as pl
from jax.experimental.pallas import tpu as pltpu
from jax.sharding import PartitionSpec as P

W = 4
WIDTH = 2 * W + 2
META_ROWS = 16
LAST = 7
LATER = ((1, 2), (2, 5), (5, LAST), (LAST, LAST + 1))
ANY = pl.BlockSpec(memory_space=pl.ANY)
HBM = pl.BlockSpec(memory_space=pltpu.HBM)
SMEM = pl.BlockSpec(memory_space=pltpu.SMEM)
VMEM = pl.BlockSpec(memory_space=pltpu.VMEM)


def find(cols_ref, counts_ref, col):
    found = jnp.int32(-1)
    for s in range(cols_ref.shape[1]):
        found = jnp.where((cols_ref[0, s] == col) & (s < counts_ref[0]), s, found)
    return found


def dot(a, b):
    return jnp.dot(a, b, preferred_element_type=jnp.float32)


def head_kernel(own, head, out, out_v, sem):
    out_v[...] = (dot(own[0], own[1]) + dot(own[1], head[...])).astype(out_v.dtype)
    copy = pltpu.make_async_copy(out_v, out.at[0, W + 1], sem)
    copy.start()
    copy.wait()


def early_kernel(total, cols, counts, next_cols, next_counts, own, band, out, table, out_v, sems):
    here = cols[0, 0]
    for s in range(next_cols.shape[1]):
        col = next_cols[0, s]
        table[0, s] = jnp.where(s < next_counts[0], lax.rem(col - here + W + total, total), -1)
        table[1, s] = find(cols, counts, col)
    table[0, next_cols.shape[1]] = lax.rem(here, 2)

    def job(k):
        col = lax.rem(here + k - W + total, total)
        return find(cols, counts, col), find(next_cols, next_counts, col) < 0

    def out_copy(k):
        return pltpu.make_async_copy(out_v.at[k], out.at[0, k], sems.at[k])

    @pl.loop(0, WIDTH)
    def _(k):
        f, active = job(k)

        @pl.when(active)
        def _():
            @pl.when(f >= 0)
            def _():
                out_v[k] = dot(own[0], own[f]).astype(out_v.dtype)

            @pl.when(f < 0)
            def _():
                out_v[k] = jnp.zeros(out_v.shape[1:], out_v.dtype)

            out_copy(k).start()

    @pl.loop(0, WIDTH)
    def _(k):
        _, active = job(k)

        @pl.when(active)
        def _():
            out_copy(k).wait()


def finish(table, own, right, slot, out_v, t):
    f = table[1, slot]

    @pl.when(f >= 0)
    def _():
        out_v[t] = (dot(own[0], own[f]) + dot(own[1], right())).astype(out_v.dtype)

    @pl.when(f < 0)
    def _():
        out_v[t] = dot(own[1], right()).astype(out_v.dtype)


def chunk_kernel(first_slot, jobs, table, own, chunk, band, out, out_v, sems):
    rows = own.shape[1]

    def out_copy(t):
        return pltpu.make_async_copy(out_v.at[t], out.at[0, table[0, first_slot + t]], sems.at[t])

    @pl.loop(0, jobs)
    def _(t):
        @pl.when(table[0, first_slot + t] >= 0)
        def _():
            finish(table, own, lambda: chunk[pl.ds(pl.multiple_of(t * rows, rows), rows)], first_slot + t, out_v, t)
            out_copy(t).start()

    @pl.loop(0, jobs)
    def _(t):
        @pl.when(table[0, first_slot + t] >= 0)
        def _():
            out_copy(t).wait()


def late_kernel(first_slot, jobs, table, own, chunk, near, band, out, base, out_v, sems):
    chunk_kernel(first_slot, jobs, table, own, chunk, band, out, out_v, sems)

    @pl.when(table[0, LAST] >= 0)
    def _():
        even = table[0, LAST + 1] == 0

        @pl.when(even)
        def _():
            finish(table, own, lambda: near[...], LAST, out_v, jobs)
            copy = pltpu.make_async_copy(out_v.at[jobs], out.at[0, table[0, LAST]], sems.at[jobs])
            copy.start()
            copy.wait()

        f = table[1, LAST]

        @pl.when(jnp.logical_not(even) & (f >= 0))
        def _():
            base[...] = dot(own[0], own[f])

        @pl.when(jnp.logical_not(even) & (f < 0))
        def _():
            base[...] = jnp.zeros(base.shape, base.dtype)


def last_kernel(table, own, chunk, base, band, out, out_v, sem):
    @pl.when((table[0, LAST] >= 0) & (table[0, LAST + 1] == 1))
    def _():
        out_v[...] = (base[...] + dot(own[1], chunk[...])).astype(out_v.dtype)
        copy = pltpu.make_async_copy(out_v, out.at[0, table[0, LAST]], sem)
        copy.start()
        copy.wait()


def pack_kernel(ranges, noted, *refs):
    cols, counts, own, _ = refs[:4]
    parts, sems = refs[4:-1], refs[-1]
    rows, lanes = own.shape[1:]
    copies = []
    for (a, b), part in zip(ranges, parts):
        for s in range(a, b):
            copies.append(pltpu.make_async_copy(own.at[s], part.at[pl.ds((s - a) * rows, rows)], sems.at[s]))
    for copy in copies:
        copy.start()
    if noted:
        lane = lax.broadcasted_iota(jnp.int32, (META_ROWS, lanes), 1)
        note = jnp.zeros((META_ROWS, lanes), jnp.int32)
        slots = cols.shape[1]
        for s in range(slots):
            note = jnp.where(lane == s, cols[0, s], note)
        note = jnp.where(lane == slots, counts[0], note)
        start = (ranges[0][1] - ranges[0][0]) * rows
        parts[0][pl.ds(start, META_ROWS)] = note.astype(jnp.float32).astype(parts[0].dtype)
    for copy in copies:
        copy.wait()


def params():
    return pltpu.CompilerParams(vmem_limit_bytes=20 * 2**20)


def pack(ranges, noted, cols, counts, own, after):
    slots, rows, lanes = own.shape
    sizes = [(b - a) * rows for a, b in ranges]
    if noted:
        sizes[0] += META_ROWS
    return pl.pallas_call(
        functools.partial(pack_kernel, ranges, noted),
        out_shape=[jax.ShapeDtypeStruct((size, lanes), own.dtype) for size in sizes],
        in_specs=[SMEM] * 2 + [HBM, ANY],
        out_specs=[VMEM] * len(sizes),
        scratch_shapes=[pltpu.SemaphoreType.DMA((slots,))],
        compiler_params=params(),
        cost_estimate=pl.CostEstimate(flops=0, bytes_accessed=8 * sum(sizes) * lanes, transcendentals=0),
    )(cols, counts, pltpu.with_memory_space_constraint(own, pltpu.HBM), after)


def call(kernel, weight, operands, spaces, scratch, extra=(), extra_specs=(), own=None):
    b = own.shape[1:]
    band = jax.ShapeDtypeStruct((1, WIDTH) + b, own.dtype)
    last = len(operands) - 1
    alone = operands[last].shape != band.shape
    return pl.pallas_call(
        kernel,
        out_shape=[band, *extra],
        in_specs=spaces,
        out_specs=[ANY, *extra_specs],
        input_output_aliases={} if alone else {last: 0},
        scratch_shapes=scratch,
        compiler_params=params(),
        cost_estimate=pl.CostEstimate(
            flops=weight * 4 * b[0] * b[0] * b[1], bytes_accessed=weight * b[0] * b[1] * 2, transcendentals=0
        ),
    )(*operands)


def per_device(tile_values, tile_cols, tile_counts):
    total = lax.axis_size("wide")
    own = tile_values
    slots, rows, lanes = own.shape
    pairs = [(i, (i - 1) % total) for i in range(total)]
    send = lambda value, some=pairs: lax.ppermute(value, "wide", some)
    tile = lambda *n: pltpu.VMEM(n + (rows, lanes), own.dtype)
    sems = lambda *n: pltpu.SemaphoreType.DMA(n)

    first = own[0]
    head = send(first)
    parts = [first]
    for ranges, after in ((LATER[:1], first), (LATER[1:3], None), (LATER[3:], head)):
        after = parts[-1] if after is None else after
        parts += pack(ranges, after is first, tile_cols, tile_counts, own, after)
    parts = parts[1:]
    chunks = [send(part) for part in parts[:-1]]
    near = send(parts[-1], pairs[1::2])
    far = send(parts[-1], pairs[0::2])

    (band,) = call(head_kernel, 12, (own, head), [VMEM] * 2, [tile(), sems()], own=own)
    got = chunks[0][(LATER[0][1] - LATER[0][0]) * rows, : slots + 1].astype(jnp.int32)
    band, table = call(
        functools.partial(early_kernel, total), 3 * WIDTH,
        (tile_cols, tile_counts, got[None, :slots], got[slots:], own, band),
        [SMEM] * 4 + [VMEM, ANY], [tile(WIDTH), sems(WIDTH)],
        [jax.ShapeDtypeStruct((2, slots + 1), jnp.int32)], [SMEM], own=own,
    )
    for (a, b), chunk in zip(LATER[:2], chunks[:2]):
        (band,) = call(
            functools.partial(chunk_kernel, a, b - a), b - a,
            (table, own, chunk, band), [SMEM] + [VMEM] * 2 + [ANY], [tile(b - a), sems(b - a)], own=own,
        )
    a, b = LATER[2]
    band, base = call(
        functools.partial(late_kernel, a, b - a), b - a + 1,
        (table, own, chunks[2], near, band), [SMEM] + [VMEM] * 3 + [ANY], [tile(b - a + 1), sems(b - a + 1)],
        [jax.ShapeDtypeStruct((rows, lanes), jnp.float32)], [VMEM], own=own,
    )
    (band,) = call(
        last_kernel, 1, (table, own, far, base, band), [SMEM] + [VMEM] * 3 + [ANY], [tile(), sems()], own=own,
    )
    return band


def solution(mesh):
    placed = (P(("groups", "wide"), None, None), P(("groups", "wide"), None), P(("groups", "wide")))
    return jax.shard_map(
        per_device,
        mesh=mesh,
        in_specs=placed,
        out_specs=P(("groups", "wide"), None, None, None),
        check_vma=False,
    )
```

```python
import functools

import jax
import jax.numpy as jnp
from jax import lax
from jax.experimental import pallas as pl
from jax.experimental.pallas import tpu as pltpu
from jax.sharding import PartitionSpec as P

W = 4
WIDTH = 2 * W + 2
META_ROWS = 16
LAST = 7
MIDDLE = ((1, 2), (2, 4), (4, 6))
ANY = pl.BlockSpec(memory_space=pl.ANY)
HBM = pl.BlockSpec(memory_space=pltpu.HBM)
SMEM = pl.BlockSpec(memory_space=pltpu.SMEM)
VMEM = pl.BlockSpec(memory_space=pltpu.VMEM)


def find(cols_ref, counts_ref, col):
    found = jnp.int32(-1)
    for s in range(cols_ref.shape[1]):
        found = jnp.where((cols_ref[0, s] == col) & (s < counts_ref[0]), s, found)
    return found


def dot(a, b):
    return jnp.dot(a, b, preferred_element_type=jnp.float32)


def head_kernel(own, head, out, out_v, sem):
    out_v[...] = (dot(own[0], own[1]) + dot(own[1], head[...])).astype(out_v.dtype)
    copy = pltpu.make_async_copy(out_v, out.at[0, W + 1], sem)
    copy.start()
    copy.wait()


def early_kernel(total, cols, counts, next_cols, next_counts, own, band, out, table, out_v, sems):
    here = cols[0, 0]
    for s in range(next_cols.shape[1]):
        col = next_cols[0, s]
        table[0, s] = jnp.where(s < next_counts[0], lax.rem(col - here + W + total, total), -1)
        table[1, s] = find(cols, counts, col)
    table[0, next_cols.shape[1]] = lax.rem(here, 2)

    def job(k):
        col = lax.rem(here + k - W + total, total)
        return find(cols, counts, col), find(next_cols, next_counts, col) < 0

    def out_copy(k):
        return pltpu.make_async_copy(out_v.at[k], out.at[0, k], sems.at[k])

    @pl.loop(0, WIDTH)
    def _(k):
        f, active = job(k)

        @pl.when(active)
        def _():
            @pl.when(f >= 0)
            def _():
                out_v[k] = dot(own[0], own[f]).astype(out_v.dtype)

            @pl.when(f < 0)
            def _():
                out_v[k] = jnp.zeros(out_v.shape[1:], out_v.dtype)

            out_copy(k).start()

    @pl.loop(0, WIDTH)
    def _(k):
        _, active = job(k)

        @pl.when(active)
        def _():
            out_copy(k).wait()


def finish(table, own, right, slot, out_v, t):
    f = table[1, slot]

    @pl.when(f >= 0)
    def _():
        out_v[t] = (dot(own[0], own[f]) + dot(own[1], right())).astype(out_v.dtype)

    @pl.when(f < 0)
    def _():
        out_v[t] = dot(own[1], right()).astype(out_v.dtype)


def chunk_kernel(first_slot, jobs, table, own, chunk, band, out, out_v, sems):
    rows = own.shape[1]

    def out_copy(t):
        return pltpu.make_async_copy(out_v.at[t], out.at[0, table[0, first_slot + t]], sems.at[t])

    @pl.loop(0, jobs)
    def _(t):
        @pl.when(table[0, first_slot + t] >= 0)
        def _():
            finish(table, own, lambda: chunk[pl.ds(pl.multiple_of(t * rows, rows), rows)], first_slot + t, out_v, t)
            out_copy(t).start()

    @pl.loop(0, jobs)
    def _(t):
        @pl.when(table[0, first_slot + t] >= 0)
        def _():
            out_copy(t).wait()


def late_kernel(first_slot, jobs, table, own, chunk, near, band, out, base, out_v, sems):
    chunk_kernel(first_slot, jobs, table, own, chunk, band, out, out_v, sems)
    rows = own.shape[1]
    upper = near.shape[0]

    @pl.when(table[0, LAST] >= 0)
    def _():
        f = table[1, LAST]
        base[...] = dot(own[1, :, upper:], chunk[jobs * rows :])

        @pl.when(f >= 0)
        def _():
            base[...] += dot(own[0], own[f])

        @pl.when(table[0, LAST + 1] == 0)
        def _():
            out_v[jobs] = (base[...] + dot(own[1, :, :upper], near[...])).astype(out_v.dtype)
            copy = pltpu.make_async_copy(out_v.at[jobs], out.at[0, table[0, LAST]], sems.at[jobs])
            copy.start()
            copy.wait()


def last_kernel(table, own, chunk, base, band, out, out_v, sem):
    @pl.when((table[0, LAST] >= 0) & (table[0, LAST + 1] == 1))
    def _():
        out_v[...] = (base[...] + dot(own[1, :, : chunk.shape[0]], chunk[...])).astype(out_v.dtype)
        copy = pltpu.make_async_copy(out_v, out.at[0, table[0, LAST]], sem)
        copy.start()
        copy.wait()


def pack_kernel(pieces, noted, *refs):
    cols, counts, own, _ = refs[:4]
    parts, sem = refs[4:-1], refs[-1]
    lanes = own.shape[2]
    copies = []
    ends = []
    for of_part, part in zip(pieces, parts):
        at = 0
        for slot, row, rows in of_part:
            copies.append(pltpu.make_async_copy(own.at[slot, pl.ds(row, rows)], part.at[pl.ds(at, rows)], sem.at[len(copies)]))
            at += rows
        ends.append(at)
    for copy in copies:
        copy.start()
    if noted:
        lane = lax.broadcasted_iota(jnp.int32, (META_ROWS, lanes), 1)
        note = jnp.zeros((META_ROWS, lanes), jnp.int32)
        slots = cols.shape[1]
        for s in range(slots):
            note = jnp.where(lane == s, cols[0, s], note)
        note = jnp.where(lane == slots, counts[0], note)
        parts[0][pl.ds(ends[0], META_ROWS)] = note.astype(jnp.float32).astype(parts[0].dtype)
    for copy in copies:
        copy.wait()


def params():
    return pltpu.CompilerParams(vmem_limit_bytes=20 * 2**20)


def pack(pieces, noted, cols, counts, own, after):
    lanes = own.shape[2]
    sizes = [sum(rows for _, _, rows in of_part) for of_part in pieces]
    if noted:
        sizes[0] += META_ROWS
    return pl.pallas_call(
        functools.partial(pack_kernel, pieces, noted),
        out_shape=[jax.ShapeDtypeStruct((size, lanes), own.dtype) for size in sizes],
        in_specs=[SMEM] * 2 + [HBM, ANY],
        out_specs=[VMEM] * len(sizes),
        scratch_shapes=[pltpu.SemaphoreType.DMA((sum(map(len, pieces)),))],
        compiler_params=params(),
        cost_estimate=pl.CostEstimate(flops=0, bytes_accessed=8 * sum(sizes) * lanes, transcendentals=0),
    )(cols, counts, pltpu.with_memory_space_constraint(own, pltpu.HBM), after)


def call(kernel, weight, operands, spaces, scratch, extra=(), extra_specs=(), own=None):
    b = own.shape[1:]
    band = jax.ShapeDtypeStruct((1, WIDTH) + b, own.dtype)
    last = len(operands) - 1
    alone = operands[last].shape != band.shape
    return pl.pallas_call(
        kernel,
        out_shape=[band, *extra],
        in_specs=spaces,
        out_specs=[ANY, *extra_specs],
        input_output_aliases={} if alone else {last: 0},
        scratch_shapes=scratch,
        compiler_params=params(),
        cost_estimate=pl.CostEstimate(
            flops=weight * 4 * b[0] * b[0] * b[1], bytes_accessed=weight * b[0] * b[1] * 2, transcendentals=0
        ),
    )(*operands)


def per_device(tile_values, tile_cols, tile_counts):
    total = lax.axis_size("wide")
    own = tile_values
    slots, rows, lanes = own.shape
    pairs = [(i, (i - 1) % total) for i in range(total)]
    send = lambda value, some=pairs: lax.ppermute(value, "wide", some)
    tile = lambda *n: pltpu.VMEM(n + (rows, lanes), own.dtype)
    sems = lambda *n: pltpu.SemaphoreType.DMA(n)

    whole = lambda a, b: tuple((s, 0, rows) for s in range(a, b))
    upper = rows // 2

    first = own[0]
    head = send(first)
    (one,) = pack([whole(1, 2)], True, tile_cols, tile_counts, own, first)
    two, three, local = pack([whole(*MIDDLE[1]), whole(*MIDDLE[2]), whole(0, slots)], False, tile_cols, tile_counts, own, one)
    (four,) = pack([whole(LAST - 1, LAST) + ((LAST, upper, rows - upper),)], False, tile_cols, tile_counts, own, head)
    chunks = [send(part) for part in (one, two, three)]
    (five,) = pack([((LAST, 0, upper),)], False, tile_cols, tile_counts, own, chunks[0])
    late = send(four)
    near = send(five, pairs[1::2])
    far = send(five, pairs[0::2])
    local = local.reshape(own.shape)

    (band,) = call(head_kernel, 12, (local, head), [VMEM] * 2, [tile(), sems()], own=own)
    got = chunks[0][rows, : slots + 1].astype(jnp.int32)
    band, table = call(
        functools.partial(early_kernel, total), 3 * WIDTH,
        (tile_cols, tile_counts, got[None, :slots], got[slots:], local, band),
        [SMEM] * 4 + [VMEM, ANY], [tile(WIDTH), sems(WIDTH)],
        [jax.ShapeDtypeStruct((2, slots + 1), jnp.int32)], [SMEM], own=own,
    )
    for (a, b), chunk in zip(MIDDLE, chunks):
        (band,) = call(
            functools.partial(chunk_kernel, a, b - a), b - a,
            (table, local, chunk, band), [SMEM] + [VMEM] * 2 + [ANY], [tile(b - a), sems(b - a)], own=own,
        )
    band, base = call(
        functools.partial(late_kernel, LAST - 1, 1), 2,
        (table, local, late, near, band), [SMEM] + [VMEM] * 3 + [ANY], [tile(2), sems(2)],
        [jax.ShapeDtypeStruct((rows, lanes), jnp.float32)], [VMEM], own=own,
    )
    (band,) = call(
        last_kernel, 1, (table, local, far, base, band), [SMEM] + [VMEM] * 3 + [ANY], [tile(), sems()], own=own,
    )
    return band


def solution(mesh):
    placed = (P(("groups", "wide"), None, None), P(("groups", "wide"), None), P(("groups", "wide")))
    return jax.shard_map(
        per_device,
        mesh=mesh,
        in_specs=placed,
        out_specs=P(("groups", "wide"), None, None, None),
        check_vma=False,
    )
```

```python
import functools

import jax
import jax.numpy as jnp
from jax import lax
from jax.experimental import pallas as pl
from jax.experimental.pallas import tpu as pltpu
from jax.sharding import PartitionSpec as P

W = 4
WIDTH = 2 * W + 2
META_ROWS = 16
LAST = 7
MIDDLE = ((1, 2), (2, 4), (4, 6))
DETOUR = 80
ANY = pl.BlockSpec(memory_space=pl.ANY)
HBM = pl.BlockSpec(memory_space=pltpu.HBM)
SMEM = pl.BlockSpec(memory_space=pltpu.SMEM)
VMEM = pl.BlockSpec(memory_space=pltpu.VMEM)


def find(cols_ref, counts_ref, col):
    found = jnp.int32(-1)
    for s in range(cols_ref.shape[1]):
        found = jnp.where((cols_ref[0, s] == col) & (s < counts_ref[0]), s, found)
    return found


def dot(a, b):
    return jnp.dot(a, b, preferred_element_type=jnp.float32)


def head_kernel(own, head, out, out_v, sem):
    out_v[...] = (dot(own[0], own[1]) + dot(own[1], head[...])).astype(out_v.dtype)
    copy = pltpu.make_async_copy(out_v, out.at[0, W + 1], sem)
    copy.start()
    copy.wait()


def early_kernel(total, cols, counts, next_cols, next_counts, own, direct, detour, band, out, table, rest, out_v, sems):
    here = cols[0, 0]

    @pl.when(here == total - 1)
    def _():
        rest[...] = detour[...]

    @pl.when(here < total - 1)
    def _():
        rest[...] = direct[...]

    for s in range(next_cols.shape[1]):
        col = next_cols[0, s]
        table[0, s] = jnp.where(s < next_counts[0], lax.rem(col - here + W + total, total), -1)
        table[1, s] = find(cols, counts, col)
    table[0, next_cols.shape[1]] = lax.rem(here, 2)

    def job(k):
        col = lax.rem(here + k - W + total, total)
        return find(cols, counts, col), find(next_cols, next_counts, col) < 0

    def out_copy(k):
        return pltpu.make_async_copy(out_v.at[k], out.at[0, k], sems.at[k])

    @pl.loop(0, WIDTH)
    def _(k):
        f, active = job(k)

        @pl.when(active)
        def _():
            @pl.when(f >= 0)
            def _():
                out_v[k] = dot(own[0], own[f]).astype(out_v.dtype)

            @pl.when(f < 0)
            def _():
                out_v[k] = jnp.zeros(out_v.shape[1:], out_v.dtype)

            out_copy(k).start()

    @pl.loop(0, WIDTH)
    def _(k):
        _, active = job(k)

        @pl.when(active)
        def _():
            out_copy(k).wait()


def finish(table, own, right, slot, out_v, t):
    f = table[1, slot]

    @pl.when(f >= 0)
    def _():
        out_v[t] = (dot(own[0], own[f]) + dot(own[1], right())).astype(out_v.dtype)

    @pl.when(f < 0)
    def _():
        out_v[t] = dot(own[1], right()).astype(out_v.dtype)


def chunk_kernel(first_slot, jobs, table, own, chunk, band, out, out_v, sems):
    rows = own.shape[1]

    def out_copy(t):
        return pltpu.make_async_copy(out_v.at[t], out.at[0, table[0, first_slot + t]], sems.at[t])

    @pl.loop(0, jobs)
    def _(t):
        @pl.when(table[0, first_slot + t] >= 0)
        def _():
            finish(table, own, lambda: chunk[pl.ds(pl.multiple_of(t * rows, rows), rows)], first_slot + t, out_v, t)
            out_copy(t).start()

    @pl.loop(0, jobs)
    def _(t):
        @pl.when(table[0, first_slot + t] >= 0)
        def _():
            out_copy(t).wait()


def late_kernel(first_slot, jobs, table, own, chunk, rest, near, band, out, base, low, out_v, sems):
    chunk_kernel(first_slot, jobs, table, own, chunk, band, out, out_v, sems)
    rows = own.shape[1]
    upper = near.shape[0]

    @pl.when(table[0, LAST] >= 0)
    def _():
        f = table[1, LAST]
        low[: low.shape[0] - DETOUR] = chunk[jobs * rows :]
        low[low.shape[0] - DETOUR :] = rest[...]
        base[...] = dot(own[1, :, upper:], low[...])

        @pl.when(f >= 0)
        def _():
            base[...] += dot(own[0], own[f])

        @pl.when(table[0, LAST + 1] == 0)
        def _():
            out_v[jobs] = (base[...] + dot(own[1, :, :upper], near[...])).astype(out_v.dtype)
            copy = pltpu.make_async_copy(out_v.at[jobs], out.at[0, table[0, LAST]], sems.at[jobs])
            copy.start()
            copy.wait()


def last_kernel(table, own, chunk, base, band, out, out_v, sem):
    @pl.when((table[0, LAST] >= 0) & (table[0, LAST + 1] == 1))
    def _():
        out_v[...] = (base[...] + dot(own[1, :, : chunk.shape[0]], chunk[...])).astype(out_v.dtype)
        copy = pltpu.make_async_copy(out_v, out.at[0, table[0, LAST]], sem)
        copy.start()
        copy.wait()


def pack_kernel(pieces, noted, *refs):
    cols, counts, own, _ = refs[:4]
    parts, sem = refs[4:-1], refs[-1]
    lanes = own.shape[2]
    copies = []
    ends = []
    for of_part, part in zip(pieces, parts):
        at = 0
        for slot, row, rows in of_part:
            copies.append(pltpu.make_async_copy(own.at[slot, pl.ds(row, rows)], part.at[pl.ds(at, rows)], sem.at[len(copies)]))
            at += rows
        ends.append(at)
    for copy in copies:
        copy.start()
    if noted:
        lane = lax.broadcasted_iota(jnp.int32, (META_ROWS, lanes), 1)
        note = jnp.zeros((META_ROWS, lanes), jnp.int32)
        slots = cols.shape[1]
        for s in range(slots):
            note = jnp.where(lane == s, cols[0, s], note)
        note = jnp.where(lane == slots, counts[0], note)
        parts[0][pl.ds(ends[0], META_ROWS)] = note.astype(jnp.float32).astype(parts[0].dtype)
    for copy in copies:
        copy.wait()


def params():
    return pltpu.CompilerParams(vmem_limit_bytes=20 * 2**20)


def pack(pieces, noted, cols, counts, own, after):
    lanes = own.shape[2]
    sizes = [sum(rows for _, _, rows in of_part) for of_part in pieces]
    if noted:
        sizes[0] += META_ROWS
    return pl.pallas_call(
        functools.partial(pack_kernel, pieces, noted),
        out_shape=[jax.ShapeDtypeStruct((size, lanes), own.dtype) for size in sizes],
        in_specs=[SMEM] * 2 + [HBM, ANY],
        out_specs=[VMEM] * len(sizes),
        scratch_shapes=[pltpu.SemaphoreType.DMA((sum(map(len, pieces)),))],
        compiler_params=params(),
        cost_estimate=pl.CostEstimate(flops=0, bytes_accessed=8 * sum(sizes) * lanes, transcendentals=0),
    )(cols, counts, pltpu.with_memory_space_constraint(own, pltpu.HBM), after)


def call(kernel, weight, operands, spaces, scratch, extra=(), extra_specs=(), own=None):
    b = own.shape[1:]
    band = jax.ShapeDtypeStruct((1, WIDTH) + b, own.dtype)
    last = len(operands) - 1
    alone = operands[last].shape != band.shape
    return pl.pallas_call(
        kernel,
        out_shape=[band, *extra],
        in_specs=spaces,
        out_specs=[ANY, *extra_specs],
        input_output_aliases={} if alone else {last: 0},
        scratch_shapes=scratch,
        compiler_params=params(),
        cost_estimate=pl.CostEstimate(
            flops=weight * 4 * b[0] * b[0] * b[1], bytes_accessed=weight * b[0] * b[1] * 2, transcendentals=0
        ),
    )(*operands)


def per_device(tile_values, tile_cols, tile_counts):
    total = lax.axis_size("wide")
    own = tile_values
    slots, rows, lanes = own.shape
    pairs = [(i, (i - 1) % total) for i in range(total)]
    send = lambda value, some=pairs: lax.ppermute(value, "wide", some)
    tile = lambda *n: pltpu.VMEM(n + (rows, lanes), own.dtype)
    sems = lambda *n: pltpu.SemaphoreType.DMA(n)

    whole = lambda a, b: tuple((s, 0, rows) for s in range(a, b))
    upper = rows // 2

    first = own[0]
    head = send(first)
    one, end = pack([whole(1, 2), ((LAST, rows - DETOUR, DETOUR),)], True, tile_cols, tile_counts, own, first)
    detour = send(send(end, [(0, 2)]), [(2, total - 1)])
    direct = send(end, pairs[1:])
    two, three, local = pack([whole(*MIDDLE[1]), whole(*MIDDLE[2]), whole(0, slots)], False, tile_cols, tile_counts, own, one)
    (four,) = pack([whole(LAST - 1, LAST) + ((LAST, upper, rows - upper - DETOUR),)], False, tile_cols, tile_counts, own, head)
    chunks = [send(part) for part in (one, two, three)]
    (five,) = pack([((LAST, 0, upper),)], False, tile_cols, tile_counts, own, chunks[0])
    late = send(four)
    near = send(five, pairs[1::2])
    far = send(five, pairs[0::2])
    local = local.reshape(own.shape)

    (band,) = call(head_kernel, 12, (local, head), [VMEM] * 2, [tile(), sems()], own=own)
    got = chunks[0][rows, : slots + 1].astype(jnp.int32)
    band, table, rest = call(
        functools.partial(early_kernel, total), 3 * WIDTH,
        (tile_cols, tile_counts, got[None, :slots], got[slots:], local, direct, detour, band),
        [SMEM] * 4 + [VMEM] * 3 + [ANY], [tile(WIDTH), sems(WIDTH)],
        [jax.ShapeDtypeStruct((2, slots + 1), jnp.int32), jax.ShapeDtypeStruct(end.shape, own.dtype)], [SMEM, VMEM], own=own,
    )
    for (a, b), chunk in zip(MIDDLE, chunks):
        (band,) = call(
            functools.partial(chunk_kernel, a, b - a), b - a,
            (table, local, chunk, band), [SMEM] + [VMEM] * 2 + [ANY], [tile(b - a), sems(b - a)], own=own,
        )
    band, base = call(
        functools.partial(late_kernel, LAST - 1, 1), 2,
        (table, local, late, rest, near, band), [SMEM] + [VMEM] * 4 + [ANY],
        [pltpu.VMEM((rows - upper, lanes), own.dtype), tile(2), sems(2)],
        [jax.ShapeDtypeStruct((rows, lanes), jnp.float32)], [VMEM], own=own,
    )
    (band,) = call(
        last_kernel, 1, (table, local, far, base, band), [SMEM] + [VMEM] * 3 + [ANY], [tile(), sems()], own=own,
    )
    return band


def solution(mesh):
    placed = (P(("groups", "wide"), None, None), P(("groups", "wide"), None), P(("groups", "wide")))
    return jax.shard_map(
        per_device,
        mesh=mesh,
        in_specs=placed,
        out_specs=P(("groups", "wide"), None, None, None),
        check_vma=False,
    )
```

```python
import functools

import jax
import jax.numpy as jnp
from jax import lax
from jax.experimental import pallas as pl
from jax.experimental.pallas import tpu as pltpu
from jax.sharding import PartitionSpec as P

W = 4
WIDTH = 2 * W + 2
META_ROWS = 16
LAST = 7
MIDDLE = ((1, 2), (2, 4), (4, 6))
DETOUR = 80
RELAY = 2
ANY = pl.BlockSpec(memory_space=pl.ANY)
HBM = pl.BlockSpec(memory_space=pltpu.HBM)
SMEM = pl.BlockSpec(memory_space=pltpu.SMEM)
VMEM = pl.BlockSpec(memory_space=pltpu.VMEM)


def find(cols_ref, counts_ref, col):
    found = jnp.int32(-1)
    for s in range(cols_ref.shape[1]):
        found = jnp.where((cols_ref[0, s] == col) & (s < counts_ref[0]), s, found)
    return found


def dot(a, b):
    return jnp.dot(a, b, preferred_element_type=jnp.float32)


def head_kernel(own, head, out, out_v, sem):
    out_v[...] = (dot(own[0], own[1]) + dot(own[1], head[...])).astype(out_v.dtype)
    copy = pltpu.make_async_copy(out_v, out.at[0, W + 1], sem)
    copy.start()
    copy.wait()


def early_kernel(total, cols, counts, next_cols, next_counts, own, band, out, table, out_v, sems):
    here = cols[0, 0]
    for s in range(next_cols.shape[1]):
        col = next_cols[0, s]
        table[0, s] = jnp.where(s < next_counts[0], lax.rem(col - here + W + total, total), -1)
        table[1, s] = find(cols, counts, col)
    table[0, next_cols.shape[1]] = lax.rem(here, 2)
    table[1, next_cols.shape[1]] = here

    def job(k):
        col = lax.rem(here + k - W + total, total)
        return find(cols, counts, col), find(next_cols, next_counts, col) < 0

    def out_copy(k):
        return pltpu.make_async_copy(out_v.at[k], out.at[0, k], sems.at[k])

    @pl.loop(0, WIDTH)
    def _(k):
        f, active = job(k)

        @pl.when(active)
        def _():
            @pl.when(f >= 0)
            def _():
                out_v[k] = dot(own[0], own[f]).astype(out_v.dtype)

            @pl.when(f < 0)
            def _():
                out_v[k] = jnp.zeros(out_v.shape[1:], out_v.dtype)

            out_copy(k).start()

    @pl.loop(0, WIDTH)
    def _(k):
        _, active = job(k)

        @pl.when(active)
        def _():
            out_copy(k).wait()


def finish(table, own, right, slot, out_v, t):
    f = table[1, slot]

    @pl.when(f >= 0)
    def _():
        out_v[t] = (dot(own[0], own[f]) + dot(own[1], right())).astype(out_v.dtype)

    @pl.when(f < 0)
    def _():
        out_v[t] = dot(own[1], right()).astype(out_v.dtype)


def chunk_kernel(first_slot, jobs, table, own, chunk, band, out, out_v, sems):
    rows = own.shape[1]

    def out_copy(t):
        return pltpu.make_async_copy(out_v.at[t], out.at[0, table[0, first_slot + t]], sems.at[t])

    @pl.loop(0, jobs)
    def _(t):
        @pl.when(table[0, first_slot + t] >= 0)
        def _():
            finish(table, own, lambda: chunk[pl.ds(pl.multiple_of(t * rows, rows), rows)], first_slot + t, out_v, t)
            out_copy(t).start()

    @pl.loop(0, jobs)
    def _(t):
        @pl.when(table[0, first_slot + t] >= 0)
        def _():
            out_copy(t).wait()


def rest_kernel(last_device, first_slot, jobs, table, own, chunk, direct, detour, band, out, rest, out_v, sems):
    @pl.when(table[1, LAST + 1] == last_device)
    def _():
        rest[...] = detour[...]

    @pl.when(table[1, LAST + 1] != last_device)
    def _():
        rest[...] = direct[...]

    chunk_kernel(first_slot, jobs, table, own, chunk, band, out, out_v, sems)


def base_kernel(first_slot, jobs, table, own, chunk, band, out, base, out_v, sems):
    f = table[1, LAST]

    @pl.when(f >= 0)
    def _():
        base[...] = dot(own[0], own[f])

    @pl.when(f < 0)
    def _():
        base[...] = jnp.zeros(base.shape, base.dtype)

    chunk_kernel(first_slot, jobs, table, own, chunk, band, out, out_v, sems)


def late_kernel(table, own, chunk, rest, near, base, band, out, low, left_v, out_v, sems):
    rows, half = left_v.shape
    fold = low.shape[0]
    k, k_last = table[0, LAST - 1], table[0, LAST]
    even = table[0, LAST + 1] == 0

    def tile(j):
        return pltpu.make_async_copy(out_v.at[j], out.at[0, table[0, LAST - 1 + j]], sems.at[j])

    left_copy = pltpu.make_async_copy(left_v, out.at[0, k_last, :, pl.ds(0, half)], sems.at[2])

    @pl.when(k >= 0)
    def _():
        finish(table, own, lambda: chunk[:rows], LAST - 1, out_v, 0)
        tile(0).start()

    @pl.when((k_last >= 0) & jnp.logical_not(even))
    def _():
        low[: fold - DETOUR] = chunk[rows:]
        low[fold - DETOUR :] = rest[...]
        left = dot(own[1, :, :fold], low[:, :half]) + dot(own[1, :, fold:], low[:, half:])
        left_v[...] = (base[:, :half] + left).astype(left_v.dtype)
        left_copy.start()
        left_copy.wait()

    @pl.when((k_last >= 0) & even)
    def _():
        out_v[1] = (base[...] + dot(own[1], near[...])).astype(out_v.dtype)
        tile(1).start()
        tile(1).wait()

    @pl.when(k >= 0)
    def _():
        tile(0).wait()


def last_kernel(table, own, chunk, base, band, out, places, out_v, sems):
    fetch = pltpu.make_async_copy(table, places, sems.at[0])
    fetch.start()
    half = chunk.shape[1]
    out_v[...] = (base[:, half:] + dot(own[1], chunk[...])).astype(out_v.dtype)
    fetch.wait()
    k = places[0, LAST]

    @pl.when((k >= 0) & (places[0, LAST + 1] == 1))
    def _():
        copy = pltpu.make_async_copy(out_v, out.at[0, k, :, pl.ds(half, half)], sems.at[1])
        copy.start()
        copy.wait()


def pack_kernel(pieces, noted, *refs):
    cols, counts, own, _ = refs[:4]
    parts, sem = refs[4:-1], refs[-1]
    copies = []
    for of_part, part in zip(pieces, parts):
        for slot, row, rows, lane, lanes, to_row, to_lane in of_part:
            copies.append(
                pltpu.make_async_copy(
                    own.at[slot, pl.ds(row, rows), pl.ds(lane, lanes)],
                    part.at[pl.ds(to_row, rows), pl.ds(to_lane, lanes)],
                    sem.at[len(copies)],
                )
            )
    for copy in copies:
        copy.start()
    if noted:
        size, lanes = parts[0].shape
        lane = lax.broadcasted_iota(jnp.int32, (META_ROWS, lanes), 1)
        note = jnp.zeros((META_ROWS, lanes), jnp.int32)
        slots = cols.shape[1]
        for s in range(slots):
            note = jnp.where(lane == s, cols[0, s], note)
        note = jnp.where(lane == slots, counts[0], note)
        parts[0][pl.ds(size - META_ROWS, META_ROWS)] = note.astype(jnp.float32).astype(parts[0].dtype)
    for copy in copies:
        copy.wait()


def params():
    return pltpu.CompilerParams(vmem_limit_bytes=20 * 2**20)


def pack(pieces, noted, cols, counts, own, after):
    shapes = []
    for of_part in pieces:
        shapes.append((max(p[5] + p[2] for p in of_part), max(p[6] + p[4] for p in of_part)))
    if noted:
        shapes[0] = (shapes[0][0] + META_ROWS, shapes[0][1])
    return pl.pallas_call(
        functools.partial(pack_kernel, pieces, noted),
        out_shape=[jax.ShapeDtypeStruct(shape, own.dtype) for shape in shapes],
        in_specs=[SMEM] * 2 + [HBM, ANY],
        out_specs=[VMEM] * len(shapes),
        scratch_shapes=[pltpu.SemaphoreType.DMA((sum(map(len, pieces)),))],
        compiler_params=params(),
        cost_estimate=pl.CostEstimate(flops=0, bytes_accessed=8 * sum(a * b for a, b in shapes), transcendentals=0),
    )(cols, counts, pltpu.with_memory_space_constraint(own, pltpu.HBM), after)


def call(kernel, weight, operands, spaces, scratch, extra=(), extra_specs=(), own=None):
    b = own.shape[1:]
    band = jax.ShapeDtypeStruct((1, WIDTH) + b, own.dtype)
    last = len(operands) - 1
    alone = operands[last].shape != band.shape
    return pl.pallas_call(
        kernel,
        out_shape=[band, *extra],
        in_specs=spaces,
        out_specs=[ANY, *extra_specs],
        input_output_aliases={} if alone else {last: 0},
        scratch_shapes=scratch,
        compiler_params=params(),
        cost_estimate=pl.CostEstimate(
            flops=weight * 4 * b[0] * b[0] * b[1], bytes_accessed=weight * b[0] * b[1] * 2, transcendentals=0
        ),
    )(*operands)


def per_device(tile_values, tile_cols, tile_counts):
    total = lax.axis_size("wide")
    own = tile_values
    slots, rows, lanes = own.shape
    pairs = [(i, (i - 1) % total) for i in range(total)]
    send = lambda value, some=pairs: lax.ppermute(value, "wide", some)
    tile = lambda *n: pltpu.VMEM(n + (rows, lanes), own.dtype)
    sems = lambda *n: pltpu.SemaphoreType.DMA(n)

    half, fold = lanes // 2, rows // 2
    whole = lambda a, b: tuple((s, 0, rows, 0, lanes, (s - a) * rows, 0) for s in range(a, b))
    folded = lambda a, b, at: tuple((LAST, j * fold + a, b - a, 0, half, at, j * half) for j in range(2))

    first = own[0]
    head = send(first)
    one, end = pack([whole(1, 2), folded(fold - DETOUR, fold, 0)], True, tile_cols, tile_counts, own, first)
    two, three, local = pack([whole(*MIDDLE[1]), whole(*MIDDLE[2]), whole(0, slots)], False, tile_cols, tile_counts, own, one)
    (four,) = pack([whole(LAST - 1, LAST) + folded(0, fold - DETOUR, rows)], False, tile_cols, tile_counts, own, head)
    chunks = [send(part) for part in (one, two, three)]
    five, seven = pack([((LAST, 0, rows, half, half, 0, 0),), whole(LAST, LAST + 1)], False, tile_cols, tile_counts, own, chunks[0])
    late = send(four)
    groups = lax.axis_size("groups")
    across = [(g * total, (g ^ 1 if groups % 2 == 0 else g) * total) for g in range(groups)]
    both = lambda value, some: lax.ppermute(value, ("groups", "wide"), some)
    direct = both(
        end,
        [(g + a, g + b) for g, _ in across for a, b in pairs[2::2]] + [(g, h + RELAY) for g, h in across],
    )
    detour = both(direct, [(h + RELAY, g + total - 1) for g, h in across])
    near = send(seven, pairs[1::2])
    far = send(five, pairs[0::2])
    local = local.reshape(own.shape)

    (band,) = call(head_kernel, 12, (local, head), [VMEM] * 2, [tile(), sems()], own=own)
    got = chunks[0][rows, : slots + 1].astype(jnp.int32)
    band, table = call(
        functools.partial(early_kernel, total), 3 * WIDTH,
        (tile_cols, tile_counts, got[None, :slots], got[slots:], local, band),
        [SMEM] * 4 + [VMEM, ANY], [tile(WIDTH), sems(WIDTH)],
        [jax.ShapeDtypeStruct((2, slots + 1), jnp.int32)], [SMEM], own=own,
    )
    a, b = MIDDLE[0]
    (band,) = call(
        functools.partial(chunk_kernel, a, b - a), b - a,
        (table, local, chunks[0], band), [SMEM] + [VMEM] * 2 + [ANY], [tile(b - a), sems(b - a)], own=own,
    )
    a, b = MIDDLE[1]
    band, rest = call(
        functools.partial(rest_kernel, total - 1, a, b - a), b - a,
        (table, local, chunks[1], direct, detour, band), [SMEM] + [VMEM] * 4 + [ANY], [tile(b - a), sems(b - a)],
        [jax.ShapeDtypeStruct(end.shape, own.dtype)], [VMEM], own=own,
    )
    a, b = MIDDLE[2]
    band, base = call(
        functools.partial(base_kernel, a, b - a), b - a,
        (table, local, chunks[2], band), [SMEM] + [VMEM] * 2 + [ANY], [tile(b - a), sems(b - a)],
        [jax.ShapeDtypeStruct((rows, lanes), jnp.float32)], [VMEM], own=own,
    )
    side = pltpu.VMEM((rows, half), own.dtype)
    (band,) = call(
        late_kernel, 2, (table, local, late, rest, near, base, band), [SMEM] + [VMEM] * 5 + [ANY],
        [pltpu.VMEM((fold, lanes), own.dtype), side, tile(2), sems(3)], own=own,
    )
    (band,) = call(
        last_kernel, 1, (table, local, far, base, band), [VMEM] * 4 + [ANY],
        [pltpu.SMEM(table.shape, table.dtype), side, sems(2)], own=own,
    )
    return band


def solution(mesh):
    placed = (P(("groups", "wide"), None, None), P(("groups", "wide"), None), P(("groups", "wide")))
    return jax.shard_map(
        per_device,
        mesh=mesh,
        in_specs=placed,
        out_specs=P(("groups", "wide"), None, None, None),
        check_vma=False,
    )
```

```python
import functools

import jax
import jax.numpy as jnp
from jax import lax
from jax.experimental import pallas as pl
from jax.experimental.pallas import tpu as pltpu
from jax.sharding import PartitionSpec as P

W = 4
WIDTH = 2 * W + 2
META_ROWS = 16
LAST = 7
MIDDLE = ((1, 2), (2, 4), (4, 6))
DETOUR = 96
RELAY = 2
ANY = pl.BlockSpec(memory_space=pl.ANY)
HBM = pl.BlockSpec(memory_space=pltpu.HBM)
SMEM = pl.BlockSpec(memory_space=pltpu.SMEM)
VMEM = pl.BlockSpec(memory_space=pltpu.VMEM)


def find(cols_ref, counts_ref, col):
    found = jnp.int32(-1)
    for s in range(cols_ref.shape[1]):
        found = jnp.where((cols_ref[0, s] == col) & (s < counts_ref[0]), s, found)
    return found


def dot(a, b):
    return jnp.dot(a, b, preferred_element_type=jnp.float32)


def head_kernel(own, head, out, out_v, sem):
    out_v[...] = (dot(own[0], own[1]) + dot(own[1], head[...])).astype(out_v.dtype)
    copy = pltpu.make_async_copy(out_v, out.at[0, W + 1], sem)
    copy.start()
    copy.wait()


def early_kernel(total, cols, counts, next_cols, next_counts, own, band, out, table, out_v, sems):
    here = cols[0, 0]
    for s in range(next_cols.shape[1]):
        col = next_cols[0, s]
        table[0, s] = jnp.where(s < next_counts[0], lax.rem(col - here + W + total, total), -1)
        table[1, s] = find(cols, counts, col)
    table[0, next_cols.shape[1]] = lax.rem(here, 2)
    table[1, next_cols.shape[1]] = here

    def job(k):
        col = lax.rem(here + k - W + total, total)
        return find(cols, counts, col), find(next_cols, next_counts, col) < 0

    def out_copy(k):
        return pltpu.make_async_copy(out_v.at[k], out.at[0, k], sems.at[k])

    @pl.loop(0, WIDTH)
    def _(k):
        f, active = job(k)

        @pl.when(active)
        def _():
            @pl.when(f >= 0)
            def _():
                out_v[k] = dot(own[0], own[f]).astype(out_v.dtype)

            @pl.when(f < 0)
            def _():
                out_v[k] = jnp.zeros(out_v.shape[1:], out_v.dtype)

            out_copy(k).start()

    @pl.loop(0, WIDTH)
    def _(k):
        _, active = job(k)

        @pl.when(active)
        def _():
            out_copy(k).wait()


def finish(table, own, right, slot, out_v, t):
    f = table[1, slot]

    @pl.when(f >= 0)
    def _():
        out_v[t] = (dot(own[0], own[f]) + dot(own[1], right())).astype(out_v.dtype)

    @pl.when(f < 0)
    def _():
        out_v[t] = dot(own[1], right()).astype(out_v.dtype)


def chunk_kernel(first_slot, jobs, table, own, chunk, band, out, out_v, sems):
    rows = own.shape[1]

    def out_copy(t):
        return pltpu.make_async_copy(out_v.at[t], out.at[0, table[0, first_slot + t]], sems.at[t])

    @pl.loop(0, jobs)
    def _(t):
        @pl.when(table[0, first_slot + t] >= 0)
        def _():
            finish(table, own, lambda: chunk[pl.ds(pl.multiple_of(t * rows, rows), rows)], first_slot + t, out_v, t)
            out_copy(t).start()

    @pl.loop(0, jobs)
    def _(t):
        @pl.when(table[0, first_slot + t] >= 0)
        def _():
            out_copy(t).wait()


def rest_kernel(last_device, first_slot, jobs, table, own, chunk, direct, detour, band, out, rest, out_v, sems):
    @pl.when(table[1, LAST + 1] == last_device)
    def _():
        rest[...] = detour[...]

    @pl.when(table[1, LAST + 1] != last_device)
    def _():
        rest[...] = direct[...]

    chunk_kernel(first_slot, jobs, table, own, chunk, band, out, out_v, sems)


def base_kernel(first_slot, jobs, table, own, chunk, band, out, base, out_v, sems):
    f = table[1, LAST]

    @pl.when(f >= 0)
    def _():
        base[...] = dot(own[0], own[f])

    @pl.when(f < 0)
    def _():
        base[...] = jnp.zeros(base.shape, base.dtype)

    chunk_kernel(first_slot, jobs, table, own, chunk, band, out, out_v, sems)


def late_kernel(table, own, chunk, rest, near, base, band, out, low, left_v, out_v, sems):
    rows, half = left_v.shape
    fold = low.shape[0]
    k, k_last = table[0, LAST - 1], table[0, LAST]
    even = table[0, LAST + 1] == 0

    def tile(j):
        return pltpu.make_async_copy(out_v.at[j], out.at[0, table[0, LAST - 1 + j]], sems.at[j])

    @pl.when(k >= 0)
    def _():
        finish(table, own, lambda: chunk[:rows], LAST - 1, out_v, 0)
        tile(0).start()

    @pl.when((k_last >= 0) & jnp.logical_not(even))
    def _():
        low[: fold - DETOUR] = chunk[rows:]
        low[fold - DETOUR :] = rest[...]
        left = dot(own[1, :, :fold], low[:, :half]) + dot(own[1, :, fold:], low[:, half:])
        left_v[...] = (base[:, :half] + left).astype(left_v.dtype)
        left_copy = pltpu.make_async_copy(left_v, out.at[0, k_last, :, pl.ds(0, half)], sems.at[2])
        left_copy.start()
        left_copy.wait()

    @pl.when((k_last >= 0) & even)
    def _():
        out_v[1] = (base[...] + dot(own[1], near[...])).astype(out_v.dtype)
        tile(1).start()
        tile(1).wait()

    @pl.when(k >= 0)
    def _():
        tile(0).wait()


def last_kernel(table, own, chunk, base, band, out, places, out_v, sems):
    fetch = pltpu.make_async_copy(table, places, sems.at[0])
    fetch.start()
    half = chunk.shape[1]
    out_v[...] = (base[:, half:] + dot(own[1], chunk[...])).astype(out_v.dtype)
    fetch.wait()
    k = places[0, LAST]

    @pl.when((k >= 0) & (places[0, LAST + 1] == 1))
    def _():
        copy = pltpu.make_async_copy(out_v, out.at[0, k, :, pl.ds(half, half)], sems.at[1])
        copy.start()
        copy.wait()


def pack_kernel(pieces, noted, *refs):
    cols, counts, own, _ = refs[:4]
    parts, sem = refs[4:-1], refs[-1]
    copies = []
    for of_part, part in zip(pieces, parts):
        for slot, row, rows, lane, lanes, to_row, to_lane in of_part:
            copies.append(
                pltpu.make_async_copy(
                    own.at[slot, pl.ds(row, rows), pl.ds(lane, lanes)],
                    part.at[pl.ds(to_row, rows), pl.ds(to_lane, lanes)],
                    sem.at[len(copies)],
                )
            )
    for copy in copies:
        copy.start()
    if noted:
        size, lanes = parts[0].shape
        lane = lax.broadcasted_iota(jnp.int32, (META_ROWS, lanes), 1)
        note = jnp.zeros((META_ROWS, lanes), jnp.int32)
        slots = cols.shape[1]
        for s in range(slots):
            note = jnp.where(lane == s, cols[0, s], note)
        note = jnp.where(lane == slots, counts[0], note)
        parts[0][pl.ds(size - META_ROWS, META_ROWS)] = note.astype(jnp.float32).astype(parts[0].dtype)
    for copy in copies:
        copy.wait()


def params():
    return pltpu.CompilerParams(vmem_limit_bytes=20 * 2**20)


def pack(pieces, noted, cols, counts, own, after):
    shapes = []
    for of_part in pieces:
        shapes.append((max(p[5] + p[2] for p in of_part), max(p[6] + p[4] for p in of_part)))
    if noted:
        shapes[0] = (shapes[0][0] + META_ROWS, shapes[0][1])
    return pl.pallas_call(
        functools.partial(pack_kernel, pieces, noted),
        out_shape=[jax.ShapeDtypeStruct(shape, own.dtype) for shape in shapes],
        in_specs=[SMEM] * 2 + [HBM, ANY],
        out_specs=[VMEM] * len(shapes),
        scratch_shapes=[pltpu.SemaphoreType.DMA((sum(map(len, pieces)),))],
        compiler_params=params(),
        cost_estimate=pl.CostEstimate(flops=0, bytes_accessed=8 * sum(a * b for a, b in shapes), transcendentals=0),
    )(cols, counts, pltpu.with_memory_space_constraint(own, pltpu.HBM), after)


def call(kernel, weight, operands, spaces, scratch, extra=(), extra_specs=(), own=None):
    b = own.shape[1:]
    band = jax.ShapeDtypeStruct((1, WIDTH) + b, own.dtype)
    last = len(operands) - 1
    alone = operands[last].shape != band.shape
    return pl.pallas_call(
        kernel,
        out_shape=[band, *extra],
        in_specs=spaces,
        out_specs=[ANY, *extra_specs],
        input_output_aliases={} if alone else {last: 0},
        scratch_shapes=scratch,
        compiler_params=params(),
        cost_estimate=pl.CostEstimate(
            flops=weight * 4 * b[0] * b[0] * b[1], bytes_accessed=weight * b[0] * b[1] * 2, transcendentals=0
        ),
    )(*operands)


def per_device(tile_values, tile_cols, tile_counts):
    total = lax.axis_size("wide")
    own = tile_values
    slots, rows, lanes = own.shape
    pairs = [(i, (i - 1) % total) for i in range(total)]
    send = lambda value, some=pairs: lax.ppermute(value, "wide", some)
    tile = lambda *n: pltpu.VMEM(n + (rows, lanes), own.dtype)
    sems = lambda *n: pltpu.SemaphoreType.DMA(n)

    half, fold = lanes // 2, rows // 2
    whole = lambda a, b: tuple((s, 0, rows, 0, lanes, (s - a) * rows, 0) for s in range(a, b))
    folded = lambda a, b, at: tuple((LAST, j * fold + a, b - a, 0, half, at, j * half) for j in range(2))

    first = own[0]
    head = send(first)
    one, end = pack([whole(1, 2), folded(fold - DETOUR, fold, 0)], True, tile_cols, tile_counts, own, first)
    two, three, local = pack([whole(*MIDDLE[1]), whole(*MIDDLE[2]), whole(0, slots)], False, tile_cols, tile_counts, own, one)
    (four,) = pack([whole(LAST - 1, LAST) + folded(0, fold - DETOUR, rows)], False, tile_cols, tile_counts, own, head)
    chunks = [send(part) for part in (one, two, three)]
    five, seven = pack([((LAST, 0, rows, half, half, 0, 0),), whole(LAST, LAST + 1)], False, tile_cols, tile_counts, own, chunks[0])
    late = send(four)
    groups = lax.axis_size("groups")
    across = [(g * total, (g ^ 1 if groups % 2 == 0 else g) * total) for g in range(groups)]
    both = lambda value, some: lax.ppermute(value, ("groups", "wide"), some)
    direct = both(
        end,
        [(g + a, g + b) for g, _ in across for a, b in pairs[2::2]] + [(g, h + RELAY) for g, h in across],
    )
    detour = both(direct, [(h + RELAY, g + total - 1) for g, h in across])
    near = send(seven, pairs[1::2])
    far = send(five, pairs[0::2])
    local = local.reshape(own.shape)

    (band,) = call(head_kernel, 12, (local, head), [VMEM] * 2, [tile(), sems()], own=own)
    got = chunks[0][rows, : slots + 1].astype(jnp.int32)
    band, table = call(
        functools.partial(early_kernel, total), 3 * WIDTH,
        (tile_cols, tile_counts, got[None, :slots], got[slots:], local, band),
        [SMEM] * 4 + [VMEM, ANY], [tile(WIDTH), sems(WIDTH)],
        [jax.ShapeDtypeStruct((2, slots + 1), jnp.int32)], [SMEM], own=own,
    )
    a, b = MIDDLE[0]
    (band,) = call(
        functools.partial(chunk_kernel, a, b - a), b - a,
        (table, local, chunks[0], band), [SMEM] + [VMEM] * 2 + [ANY], [tile(b - a), sems(b - a)], own=own,
    )
    a, b = MIDDLE[1]
    band, rest = call(
        functools.partial(rest_kernel, total - 1, a, b - a), b - a,
        (table, local, chunks[1], direct, detour, band), [SMEM] + [VMEM] * 4 + [ANY], [tile(b - a), sems(b - a)],
        [jax.ShapeDtypeStruct(end.shape, own.dtype)], [VMEM], own=own,
    )
    a, b = MIDDLE[2]
    band, base = call(
        functools.partial(base_kernel, a, b - a), b - a,
        (table, local, chunks[2], band), [SMEM] + [VMEM] * 2 + [ANY], [tile(b - a), sems(b - a)],
        [jax.ShapeDtypeStruct((rows, lanes), jnp.float32)], [VMEM], own=own,
    )
    side = pltpu.VMEM((rows, half), own.dtype)
    (band,) = call(
        late_kernel, 2, (table, local, late, rest, near, base, band), [SMEM] + [VMEM] * 5 + [ANY],
        [pltpu.VMEM((fold, lanes), own.dtype), side, tile(2), sems(3)], own=own,
    )
    (band,) = call(
        last_kernel, 1, (table, local, far, base, band), [VMEM] * 4 + [ANY],
        [pltpu.SMEM(table.shape, table.dtype), side, sems(2)], own=own,
    )
    return band


def solution(mesh):
    placed = (P(("groups", "wide"), None, None), P(("groups", "wide"), None), P(("groups", "wide")))
    return jax.shard_map(
        per_device,
        mesh=mesh,
        in_specs=placed,
        out_specs=P(("groups", "wide"), None, None, None),
        check_vma=False,
    )
```

```python
import functools

import jax
import jax.numpy as jnp
from jax import lax
from jax.experimental import pallas as pl
from jax.experimental.pallas import tpu as pltpu
from jax.sharding import PartitionSpec as P

W = 4
WIDTH = 2 * W + 2
META_ROWS = 16
LAST = 7
MIDDLE = ((1, 2), (2, 4), (4, 6))
DETOUR = 96
RELAY = 2
ANY = pl.BlockSpec(memory_space=pl.ANY)
HBM = pl.BlockSpec(memory_space=pltpu.HBM)
SMEM = pl.BlockSpec(memory_space=pltpu.SMEM)
VMEM = pl.BlockSpec(memory_space=pltpu.VMEM)


def find(cols_ref, counts_ref, col):
    found = jnp.int32(-1)
    for s in range(cols_ref.shape[1]):
        found = jnp.where((cols_ref[0, s] == col) & (s < counts_ref[0]), s, found)
    return found


def dot(a, b):
    return jnp.dot(a, b, preferred_element_type=jnp.float32)


def head_kernel(own, head, out, out_v, sem):
    out_v[...] = (dot(own[0], own[1]) + dot(own[1], head[...])).astype(out_v.dtype)
    copy = pltpu.make_async_copy(out_v, out.at[0, W + 1], sem)
    copy.start()
    copy.wait()


def early_kernel(total, cols, counts, next_cols, next_counts, own, band, out, table, place, out_v, sems):
    here = cols[0, 0]
    for s in range(next_cols.shape[1]):
        col = next_cols[0, s]
        table[0, s] = jnp.where(s < next_counts[0], lax.rem(col - here + W + total, total), -1)
        table[1, s] = find(cols, counts, col)
    table[0, next_cols.shape[1]] = lax.rem(here, 2)
    table[1, next_cols.shape[1]] = here
    place[...] = jnp.full(place.shape, jnp.where(lax.rem(here, 2) == 1, table[0, LAST], -1), jnp.int32)

    def job(k):
        col = lax.rem(here + k - W + total, total)
        return find(cols, counts, col), find(next_cols, next_counts, col) < 0

    def out_copy(k):
        return pltpu.make_async_copy(out_v.at[k], out.at[0, k], sems.at[k])

    @pl.loop(0, WIDTH)
    def _(k):
        f, active = job(k)

        @pl.when(active)
        def _():
            @pl.when(f >= 0)
            def _():
                out_v[k] = dot(own[0], own[f]).astype(out_v.dtype)

            @pl.when(f < 0)
            def _():
                out_v[k] = jnp.zeros(out_v.shape[1:], out_v.dtype)

            out_copy(k).start()

    @pl.loop(0, WIDTH)
    def _(k):
        _, active = job(k)

        @pl.when(active)
        def _():
            out_copy(k).wait()


def finish(table, own, right, slot, out_v, t):
    f = table[1, slot]

    @pl.when(f >= 0)
    def _():
        out_v[t] = (dot(own[0], own[f]) + dot(own[1], right())).astype(out_v.dtype)

    @pl.when(f < 0)
    def _():
        out_v[t] = dot(own[1], right()).astype(out_v.dtype)


def chunk_kernel(first_slot, jobs, table, own, chunk, band, out, out_v, sems):
    rows = own.shape[1]

    def out_copy(t):
        return pltpu.make_async_copy(out_v.at[t], out.at[0, table[0, first_slot + t]], sems.at[t])

    @pl.loop(0, jobs)
    def _(t):
        @pl.when(table[0, first_slot + t] >= 0)
        def _():
            finish(table, own, lambda: chunk[pl.ds(pl.multiple_of(t * rows, rows), rows)], first_slot + t, out_v, t)
            out_copy(t).start()

    @pl.loop(0, jobs)
    def _(t):
        @pl.when(table[0, first_slot + t] >= 0)
        def _():
            out_copy(t).wait()


def rest_kernel(last_device, first_slot, jobs, table, own, chunk, direct, detour, band, out, rest, out_v, sems):
    @pl.when(table[1, LAST + 1] == last_device)
    def _():
        rest[...] = detour[...]

    @pl.when(table[1, LAST + 1] != last_device)
    def _():
        rest[...] = direct[...]

    chunk_kernel(first_slot, jobs, table, own, chunk, band, out, out_v, sems)


def base_kernel(first_slot, jobs, table, own, chunk, band, out, base, out_v, sems):
    f = table[1, LAST]

    @pl.when(f >= 0)
    def _():
        base[...] = dot(own[0], own[f])

    @pl.when(f < 0)
    def _():
        base[...] = jnp.zeros(base.shape, base.dtype)

    chunk_kernel(first_slot, jobs, table, own, chunk, band, out, out_v, sems)


def late_kernel(table, own, chunk, rest, near, base, band, out, low, left_v, out_v, sems):
    rows, half = left_v.shape
    fold = low.shape[0]
    k, k_last = table[0, LAST - 1], table[0, LAST]
    even = table[0, LAST + 1] == 0

    def tile(j):
        return pltpu.make_async_copy(out_v.at[j], out.at[0, table[0, LAST - 1 + j]], sems.at[j])

    @pl.when(k >= 0)
    def _():
        finish(table, own, lambda: chunk[:rows], LAST - 1, out_v, 0)
        tile(0).start()

    @pl.when((k_last >= 0) & jnp.logical_not(even))
    def _():
        low[: fold - DETOUR] = chunk[rows:]
        low[fold - DETOUR :] = rest[...]
        left = dot(own[1, :, :fold], low[:, :half]) + dot(own[1, :, fold:], low[:, half:])
        left_v[...] = (base[:, :half] + left).astype(left_v.dtype)
        left_copy = pltpu.make_async_copy(left_v, out.at[0, k_last, :, pl.ds(0, half)], sems.at[2])
        left_copy.start()
        left_copy.wait()

    @pl.when((k_last >= 0) & even)
    def _():
        out_v[1] = (base[...] + dot(own[1], near[...])).astype(out_v.dtype)
        tile(1).start()
        tile(1).wait()

    @pl.when(k >= 0)
    def _():
        tile(0).wait()


def last_kernel(place, own, chunk, base, band, out, out_v, sem):
    k = jnp.max(place[...])
    half = chunk.shape[1]
    out_v[...] = (base[:, half:] + dot(own[1], chunk[...])).astype(out_v.dtype)

    @pl.when(k >= 0)
    def _():
        copy = pltpu.make_async_copy(out_v, out.at[0, k, :, pl.ds(half, half)], sem)
        copy.start()
        copy.wait()


def pack_kernel(pieces, noted, *refs):
    cols, counts, own, _ = refs[:4]
    parts, sem = refs[4:-1], refs[-1]
    copies = []
    for of_part, part in zip(pieces, parts):
        for slot, row, rows, lane, lanes, to_row, to_lane in of_part:
            copies.append(
                pltpu.make_async_copy(
                    own.at[slot, pl.ds(row, rows), pl.ds(lane, lanes)],
                    part.at[pl.ds(to_row, rows), pl.ds(to_lane, lanes)],
                    sem.at[len(copies)],
                )
            )
    for copy in copies:
        copy.start()
    if noted:
        size, lanes = parts[0].shape
        lane = lax.broadcasted_iota(jnp.int32, (META_ROWS, lanes), 1)
        note = jnp.zeros((META_ROWS, lanes), jnp.int32)
        slots = cols.shape[1]
        for s in range(slots):
            note = jnp.where(lane == s, cols[0, s], note)
        note = jnp.where(lane == slots, counts[0], note)
        parts[0][pl.ds(size - META_ROWS, META_ROWS)] = note.astype(jnp.float32).astype(parts[0].dtype)
    for copy in copies:
        copy.wait()


def params():
    return pltpu.CompilerParams(vmem_limit_bytes=20 * 2**20)


def pack(pieces, noted, cols, counts, own, after):
    shapes = []
    for of_part in pieces:
        shapes.append((max(p[5] + p[2] for p in of_part), max(p[6] + p[4] for p in of_part)))
    if noted:
        shapes[0] = (shapes[0][0] + META_ROWS, shapes[0][1])
    return pl.pallas_call(
        functools.partial(pack_kernel, pieces, noted),
        out_shape=[jax.ShapeDtypeStruct(shape, own.dtype) for shape in shapes],
        in_specs=[SMEM] * 2 + [HBM, ANY],
        out_specs=[VMEM] * len(shapes),
        scratch_shapes=[pltpu.SemaphoreType.DMA((sum(map(len, pieces)),))],
        compiler_params=params(),
        cost_estimate=pl.CostEstimate(flops=0, bytes_accessed=8 * sum(a * b for a, b in shapes), transcendentals=0),
    )(cols, counts, pltpu.with_memory_space_constraint(own, pltpu.HBM), after)


def call(kernel, weight, operands, spaces, scratch, extra=(), extra_specs=(), own=None):
    b = own.shape[1:]
    band = jax.ShapeDtypeStruct((1, WIDTH) + b, own.dtype)
    last = len(operands) - 1
    alone = operands[last].shape != band.shape
    return pl.pallas_call(
        kernel,
        out_shape=[band, *extra],
        in_specs=spaces,
        out_specs=[ANY, *extra_specs],
        input_output_aliases={} if alone else {last: 0},
        scratch_shapes=scratch,
        compiler_params=params(),
        cost_estimate=pl.CostEstimate(
            flops=weight * 4 * b[0] * b[0] * b[1], bytes_accessed=weight * b[0] * b[1] * 2, transcendentals=0
        ),
    )(*operands)


def per_device(tile_values, tile_cols, tile_counts):
    total = lax.axis_size("wide")
    own = tile_values
    slots, rows, lanes = own.shape
    pairs = [(i, (i - 1) % total) for i in range(total)]
    send = lambda value, some=pairs: lax.ppermute(value, "wide", some)
    tile = lambda *n: pltpu.VMEM(n + (rows, lanes), own.dtype)
    sems = lambda *n: pltpu.SemaphoreType.DMA(n)

    half, fold = lanes // 2, rows // 2
    whole = lambda a, b: tuple((s, 0, rows, 0, lanes, (s - a) * rows, 0) for s in range(a, b))
    folded = lambda a, b, at: tuple((LAST, j * fold + a, b - a, 0, half, at, j * half) for j in range(2))

    first = own[0]
    head = send(first)
    one, end = pack([whole(1, 2), folded(fold - DETOUR, fold, 0)], True, tile_cols, tile_counts, own, first)
    two, three, local = pack([whole(*MIDDLE[1]), whole(*MIDDLE[2]), whole(0, slots)], False, tile_cols, tile_counts, own, one)
    (four,) = pack([whole(LAST - 1, LAST) + folded(0, fold - DETOUR, rows)], False, tile_cols, tile_counts, own, head)
    chunks = [send(part) for part in (one, two, three)]
    five, seven = pack([((LAST, 0, rows, half, half, 0, 0),), whole(LAST, LAST + 1)], False, tile_cols, tile_counts, own, chunks[0])
    late = send(four)
    groups = lax.axis_size("groups")
    across = [(g * total, (g ^ 1 if groups % 2 == 0 else g) * total) for g in range(groups)]
    both = lambda value, some: lax.ppermute(value, ("groups", "wide"), some)
    direct = both(
        end,
        [(g + a, g + b) for g, _ in across for a, b in pairs[2::2]] + [(g, h + RELAY) for g, h in across],
    )
    detour = both(direct, [(h + RELAY, g + total - 1) for g, h in across])
    near = send(seven, pairs[1::2])
    far = send(five, pairs[0::2])
    local = local.reshape(own.shape)

    (band,) = call(head_kernel, 12, (local, head), [VMEM] * 2, [tile(), sems()], own=own)
    got = chunks[0][rows, : slots + 1].astype(jnp.int32)
    band, table, place = call(
        functools.partial(early_kernel, total), 3 * WIDTH,
        (tile_cols, tile_counts, got[None, :slots], got[slots:], local, band),
        [SMEM] * 4 + [VMEM, ANY], [tile(WIDTH), sems(WIDTH)],
        [jax.ShapeDtypeStruct((2, slots + 1), jnp.int32), jax.ShapeDtypeStruct((8, 128), jnp.int32)], [SMEM, VMEM], own=own,
    )
    a, b = MIDDLE[0]
    (band,) = call(
        functools.partial(chunk_kernel, a, b - a), b - a,
        (table, local, chunks[0], band), [SMEM] + [VMEM] * 2 + [ANY], [tile(b - a), sems(b - a)], own=own,
    )
    a, b = MIDDLE[1]
    band, rest = call(
        functools.partial(rest_kernel, total - 1, a, b - a), b - a,
        (table, local, chunks[1], direct, detour, band), [SMEM] + [VMEM] * 4 + [ANY], [tile(b - a), sems(b - a)],
        [jax.ShapeDtypeStruct(end.shape, own.dtype)], [VMEM], own=own,
    )
    a, b = MIDDLE[2]
    band, base = call(
        functools.partial(base_kernel, a, b - a), b - a,
        (table, local, chunks[2], band), [SMEM] + [VMEM] * 2 + [ANY], [tile(b - a), sems(b - a)],
        [jax.ShapeDtypeStruct((rows, lanes), jnp.float32)], [VMEM], own=own,
    )
    side = pltpu.VMEM((rows, half), own.dtype)
    (band,) = call(
        late_kernel, 2, (table, local, late, rest, near, base, band), [SMEM] + [VMEM] * 5 + [ANY],
        [pltpu.VMEM((fold, lanes), own.dtype), side, tile(2), sems(3)], own=own,
    )
    (band,) = call(
        last_kernel, 1, (place, local, far, base, band), [VMEM] * 4 + [ANY], [side, sems()], own=own,
    )
    return band


def solution(mesh):
    placed = (P(("groups", "wide"), None, None), P(("groups", "wide"), None), P(("groups", "wide")))
    return jax.shard_map(
        per_device,
        mesh=mesh,
        in_specs=placed,
        out_specs=P(("groups", "wide"), None, None, None),
        check_vma=False,
    )
```

```python
import functools

import jax
import jax.numpy as jnp
from jax import lax
from jax.experimental import pallas as pl
from jax.experimental.pallas import tpu as pltpu
from jax.sharding import PartitionSpec as P

W = 4
WIDTH = 2 * W + 2
META_ROWS = 16
LAST = 7
MIDDLE = ((1, 2), (2, 4), (4, 6))
BLOCKS = (48, 64)
DETOUR = sum(BLOCKS)
ANY = pl.BlockSpec(memory_space=pl.ANY)
HBM = pl.BlockSpec(memory_space=pltpu.HBM)
SMEM = pl.BlockSpec(memory_space=pltpu.SMEM)
VMEM = pl.BlockSpec(memory_space=pltpu.VMEM)


def find(cols_ref, counts_ref, col):
    found = jnp.int32(-1)
    for s in range(cols_ref.shape[1]):
        found = jnp.where((cols_ref[0, s] == col) & (s < counts_ref[0]), s, found)
    return found


def dot(a, b):
    return jnp.dot(a, b, preferred_element_type=jnp.float32)


def head_kernel(own, head, out, out_v, sem):
    out_v[...] = (dot(own[0], own[1]) + dot(own[1], head[...])).astype(out_v.dtype)
    copy = pltpu.make_async_copy(out_v, out.at[0, W + 1], sem)
    copy.start()
    copy.wait()


def early_kernel(total, cols, counts, next_cols, next_counts, own, band, out, table, place, out_v, sems):
    here = cols[0, 0]
    for s in range(next_cols.shape[1]):
        col = next_cols[0, s]
        table[0, s] = jnp.where(s < next_counts[0], lax.rem(col - here + W + total, total), -1)
        table[1, s] = find(cols, counts, col)
    table[0, next_cols.shape[1]] = lax.rem(here, 2)
    table[1, next_cols.shape[1]] = here
    place[...] = jnp.full(place.shape, jnp.where(lax.rem(here, 2) == 1, table[0, LAST], -1), jnp.int32)

    def job(k):
        col = lax.rem(here + k - W + total, total)
        return find(cols, counts, col), find(next_cols, next_counts, col) < 0

    def out_copy(k):
        return pltpu.make_async_copy(out_v.at[k], out.at[0, k], sems.at[k])

    @pl.loop(0, WIDTH)
    def _(k):
        f, active = job(k)

        @pl.when(active)
        def _():
            @pl.when(f >= 0)
            def _():
                out_v[k] = dot(own[0], own[f]).astype(out_v.dtype)

            @pl.when(f < 0)
            def _():
                out_v[k] = jnp.zeros(out_v.shape[1:], out_v.dtype)

            out_copy(k).start()

    @pl.loop(0, WIDTH)
    def _(k):
        _, active = job(k)

        @pl.when(active)
        def _():
            out_copy(k).wait()


def finish(table, own, right, slot, out_v, t):
    f = table[1, slot]

    @pl.when(f >= 0)
    def _():
        out_v[t] = (dot(own[0], own[f]) + dot(own[1], right())).astype(out_v.dtype)

    @pl.when(f < 0)
    def _():
        out_v[t] = dot(own[1], right()).astype(out_v.dtype)


def chunk_kernel(first_slot, jobs, table, own, chunk, band, out, out_v, sems):
    rows = own.shape[1]

    def out_copy(t):
        return pltpu.make_async_copy(out_v.at[t], out.at[0, table[0, first_slot + t]], sems.at[t])

    @pl.loop(0, jobs)
    def _(t):
        @pl.when(table[0, first_slot + t] >= 0)
        def _():
            finish(table, own, lambda: chunk[pl.ds(pl.multiple_of(t * rows, rows), rows)], first_slot + t, out_v, t)
            out_copy(t).start()

    @pl.loop(0, jobs)
    def _(t):
        @pl.when(table[0, first_slot + t] >= 0)
        def _():
            out_copy(t).wait()


def rest_kernel(last_device, first_slot, jobs, table, own, chunk, direct, detour, band, out, rest, out_v, sems):
    here = table[1, LAST + 1]

    @pl.when(here == last_device)
    def _():
        rest[...] = detour[...]

    @pl.when(here != last_device)
    def _():
        rest[...] = direct[...]

    chunk_kernel(first_slot, jobs, table, own, chunk, band, out, out_v, sems)


def base_kernel(first_slot, jobs, table, own, chunk, band, out, base, out_v, sems):
    f = table[1, LAST]

    @pl.when(f >= 0)
    def _():
        base[...] = dot(own[0], own[f])

    @pl.when(f < 0)
    def _():
        base[...] = jnp.zeros(base.shape, base.dtype)

    chunk_kernel(first_slot, jobs, table, own, chunk, band, out, out_v, sems)


def late_kernel(last_device, table, own, chunk, rest, direct, detour, near, base, band, out, low, left_v, out_v, sems):
    rows, half = left_v.shape
    fold = low.shape[0]
    k, k_last = table[0, LAST - 1], table[0, LAST]
    even = table[0, LAST + 1] == 0

    def tile(j):
        return pltpu.make_async_copy(out_v.at[j], out.at[0, table[0, LAST - 1 + j]], sems.at[j])

    @pl.when(k >= 0)
    def _():
        finish(table, own, lambda: chunk[:rows], LAST - 1, out_v, 0)
        tile(0).start()

    @pl.when((k_last >= 0) & jnp.logical_not(even))
    def _():
        low[: fold - DETOUR] = chunk[rows:]
        low[fold - DETOUR : fold - BLOCKS[1]] = rest[...]
        here = table[1, LAST + 1]
        around = (here == last_device) | (here == 3)

        @pl.when(around)
        def _():
            low[fold - BLOCKS[1] :] = detour[...]

        @pl.when(jnp.logical_not(around))
        def _():
            low[fold - BLOCKS[1] :] = direct[...]

        left = dot(own[1, :, :fold], low[:, :half]) + dot(own[1, :, fold:], low[:, half:])
        left_v[...] = (base[:, :half] + left).astype(left_v.dtype)
        left_copy = pltpu.make_async_copy(left_v, out.at[0, k_last, :, pl.ds(0, half)], sems.at[2])
        left_copy.start()
        left_copy.wait()

    @pl.when((k_last >= 0) & even)
    def _():
        out_v[1] = (base[...] + dot(own[1], near[...])).astype(out_v.dtype)
        tile(1).start()
        tile(1).wait()

    @pl.when(k >= 0)
    def _():
        tile(0).wait()


def last_kernel(place, own, chunk, base, band, out, out_v, sem):
    k = jnp.max(place[...])
    half = chunk.shape[1]
    out_v[...] = (base[:, half:] + dot(own[1], chunk[...])).astype(out_v.dtype)

    @pl.when(k >= 0)
    def _():
        copy = pltpu.make_async_copy(out_v, out.at[0, k, :, pl.ds(half, half)], sem)
        copy.start()
        copy.wait()


def pack_kernel(pieces, noted, *refs):
    cols, counts, own, _ = refs[:4]
    parts, sem = refs[4:-1], refs[-1]
    copies = []
    for of_part, part in zip(pieces, parts):
        for slot, row, rows, lane, lanes, to_row, to_lane in of_part:
            copies.append(
                pltpu.make_async_copy(
                    own.at[slot, pl.ds(row, rows), pl.ds(lane, lanes)],
                    part.at[pl.ds(to_row, rows), pl.ds(to_lane, lanes)],
                    sem.at[len(copies)],
                )
            )
    for copy in copies:
        copy.start()
    if noted:
        size, lanes = parts[0].shape
        lane = lax.broadcasted_iota(jnp.int32, (META_ROWS, lanes), 1)
        note = jnp.zeros((META_ROWS, lanes), jnp.int32)
        slots = cols.shape[1]
        for s in range(slots):
            note = jnp.where(lane == s, cols[0, s], note)
        note = jnp.where(lane == slots, counts[0], note)
        parts[0][pl.ds(size - META_ROWS, META_ROWS)] = note.astype(jnp.float32).astype(parts[0].dtype)
    for copy in copies:
        copy.wait()


def params():
    return pltpu.CompilerParams(vmem_limit_bytes=20 * 2**20)


def pack(pieces, noted, cols, counts, own, after):
    shapes = []
    for of_part in pieces:
        shapes.append((max(p[5] + p[2] for p in of_part), max(p[6] + p[4] for p in of_part)))
    if noted:
        shapes[0] = (shapes[0][0] + META_ROWS, shapes[0][1])
    return pl.pallas_call(
        functools.partial(pack_kernel, pieces, noted),
        out_shape=[jax.ShapeDtypeStruct(shape, own.dtype) for shape in shapes],
        in_specs=[SMEM] * 2 + [HBM, ANY],
        out_specs=[VMEM] * len(shapes),
        scratch_shapes=[pltpu.SemaphoreType.DMA((sum(map(len, pieces)),))],
        compiler_params=params(),
        cost_estimate=pl.CostEstimate(flops=0, bytes_accessed=8 * sum(a * b for a, b in shapes), transcendentals=0),
    )(cols, counts, pltpu.with_memory_space_constraint(own, pltpu.HBM), after)


def call(kernel, weight, operands, spaces, scratch, extra=(), extra_specs=(), own=None):
    b = own.shape[1:]
    band = jax.ShapeDtypeStruct((1, WIDTH) + b, own.dtype)
    last = len(operands) - 1
    alone = operands[last].shape != band.shape
    return pl.pallas_call(
        kernel,
        out_shape=[band, *extra],
        in_specs=spaces,
        out_specs=[ANY, *extra_specs],
        input_output_aliases={} if alone else {last: 0},
        scratch_shapes=scratch,
        compiler_params=params(),
        cost_estimate=pl.CostEstimate(
            flops=weight * 4 * b[0] * b[0] * b[1], bytes_accessed=weight * b[0] * b[1] * 2, transcendentals=0
        ),
    )(*operands)


def per_device(tile_values, tile_cols, tile_counts):
    total = lax.axis_size("wide")
    own = tile_values
    slots, rows, lanes = own.shape
    pairs = [(i, (i - 1) % total) for i in range(total)]
    send = lambda value, some=pairs: lax.ppermute(value, "wide", some)
    tile = lambda *n: pltpu.VMEM(n + (rows, lanes), own.dtype)
    sems = lambda *n: pltpu.SemaphoreType.DMA(n)

    half, fold = lanes // 2, rows // 2
    whole = lambda a, b: tuple((s, 0, rows, 0, lanes, (s - a) * rows, 0) for s in range(a, b))
    folded = lambda a, b, at: tuple((LAST, j * fold + a, b - a, 0, half, at, j * half) for j in range(2))

    first = own[0]
    head = send(first)
    cut = fold - BLOCKS[1]
    one, end_a = pack([whole(1, 2), folded(fold - DETOUR, cut, 0)], True, tile_cols, tile_counts, own, first)
    two, local = pack([whole(*MIDDLE[1]), whole(0, slots)], False, tile_cols, tile_counts, own, one)
    three, end_b = pack([whole(*MIDDLE[2]), folded(cut, fold, 0)], False, tile_cols, tile_counts, own, head)
    chunks = [send(part) for part in (one, two, three)]
    four, five, seven = pack(
        [whole(LAST - 1, LAST) + folded(0, fold - DETOUR, rows), ((LAST, 0, rows, half, half, 0, 0),), whole(LAST, LAST + 1)],
        False, tile_cols, tile_counts, own, chunks[0],
    )
    late = send(four)
    groups = lax.axis_size("groups")
    across = [(g * total, (g ^ 1 if groups % 2 == 0 else g) * total) for g in range(groups)]
    both = lambda value, some: lax.ppermute(value, ("groups", "wide"), some)
    straight = [(g * total + i, g * total + j) for g in range(groups) for i, j in pairs[2::2]]
    shift = lambda some: [(g + i, h + j) for g, h in across for i, j in some]
    direct_a = both(end_a, straight + shift([(0, 2)]))
    direct_b = both(end_b, [p for p in straight if p[0] % total != 4] + shift([(0, 2), (4, 6)]))
    detour_a = both(direct_a, shift([(2, total - 1)]))
    detour_b = both(direct_b, shift([(2, total - 1), (6, 3)]))
    near = send(seven, pairs[1::2])
    far = send(five, pairs[0::2])
    local = local.reshape(own.shape)

    (band,) = call(head_kernel, 12, (local, head), [VMEM] * 2, [tile(), sems()], own=own)
    got = chunks[0][rows, : slots + 1].astype(jnp.int32)
    band, table, place = call(
        functools.partial(early_kernel, total), 3 * WIDTH,
        (tile_cols, tile_counts, got[None, :slots], got[slots:], local, band),
        [SMEM] * 4 + [VMEM, ANY], [tile(WIDTH), sems(WIDTH)],
        [jax.ShapeDtypeStruct((2, slots + 1), jnp.int32), jax.ShapeDtypeStruct((8, 128), jnp.int32)], [SMEM, VMEM], own=own,
    )
    a, b = MIDDLE[0]
    band, base = call(
        functools.partial(base_kernel, a, b - a), b - a,
        (table, local, chunks[0], band), [SMEM] + [VMEM] * 2 + [ANY], [tile(b - a), sems(b - a)],
        [jax.ShapeDtypeStruct((rows, lanes), jnp.float32)], [VMEM], own=own,
    )
    a, b = MIDDLE[1]
    band, rest = call(
        functools.partial(rest_kernel, total - 1, a, b - a), b - a,
        (table, local, chunks[1], direct_a, detour_a, band), [SMEM] + [VMEM] * 4 + [ANY], [tile(b - a), sems(b - a)],
        [jax.ShapeDtypeStruct((BLOCKS[0], lanes), own.dtype)], [VMEM], own=own,
    )
    a, b = MIDDLE[2]
    (band,) = call(
        functools.partial(chunk_kernel, a, b - a), b - a,
        (table, local, chunks[2], band), [SMEM] + [VMEM] * 2 + [ANY], [tile(b - a), sems(b - a)], own=own,
    )
    side = pltpu.VMEM((rows, half), own.dtype)
    (band,) = call(
        functools.partial(late_kernel, total - 1), 2,
        (table, local, late, rest, direct_b, detour_b, near, base, band), [SMEM] + [VMEM] * 7 + [ANY],
        [pltpu.VMEM((fold, lanes), own.dtype), side, tile(2), sems(3)], own=own,
    )
    (band,) = call(
        last_kernel, 1, (place, local, far, base, band), [VMEM] * 4 + [ANY], [side, sems()], own=own,
    )
    return band


def solution(mesh):
    placed = (P(("groups", "wide"), None, None), P(("groups", "wide"), None), P(("groups", "wide")))
    return jax.shard_map(
        per_device,
        mesh=mesh,
        in_specs=placed,
        out_specs=P(("groups", "wide"), None, None, None),
        check_vma=False,
    )
```

```python
import functools

import jax
import jax.numpy as jnp
from jax import lax
from jax.experimental import pallas as pl
from jax.experimental.pallas import tpu as pltpu
from jax.sharding import PartitionSpec as P

W = 4
WIDTH = 2 * W + 2
META_ROWS = 16
LAST = 7
MIDDLE = ((1, 2), (2, 4), (4, 6))
BLOCKS = (48, 64)
DETOUR = sum(BLOCKS)
ANY = pl.BlockSpec(memory_space=pl.ANY)
HBM = pl.BlockSpec(memory_space=pltpu.HBM)
SMEM = pl.BlockSpec(memory_space=pltpu.SMEM)
VMEM = pl.BlockSpec(memory_space=pltpu.VMEM)


def find(cols_ref, counts_ref, col):
    found = jnp.int32(-1)
    for s in range(cols_ref.shape[1]):
        found = jnp.where((cols_ref[0, s] == col) & (s < counts_ref[0]), s, found)
    return found


def dot(a, b):
    return jnp.dot(a, b, preferred_element_type=jnp.float32)


def head_kernel(own, head, out, out_v, sem):
    out_v[...] = (dot(own[0], own[1]) + dot(own[1], head[...])).astype(out_v.dtype)
    copy = pltpu.make_async_copy(out_v, out.at[0, W + 1], sem)
    copy.start()
    copy.wait()


def early_kernel(total, cols, counts, next_cols, next_counts, own, band, out, table, place, out_v, sems):
    here = cols[0, 0]
    for s in range(next_cols.shape[1]):
        col = next_cols[0, s]
        table[0, s] = jnp.where(s < next_counts[0], lax.rem(col - here + W + total, total), -1)
        table[1, s] = find(cols, counts, col)
    table[0, next_cols.shape[1]] = lax.rem(here, 2)
    table[1, next_cols.shape[1]] = here
    place[...] = jnp.full(place.shape, jnp.where(lax.rem(here, 2) == 1, table[0, LAST], -1), jnp.int32)

    def job(k):
        col = lax.rem(here + k - W + total, total)
        return find(cols, counts, col), find(next_cols, next_counts, col) < 0

    def out_copy(k):
        return pltpu.make_async_copy(out_v.at[k], out.at[0, k], sems.at[k])

    @pl.loop(0, WIDTH)
    def _(k):
        f, active = job(k)

        @pl.when(active)
        def _():
            @pl.when(f >= 0)
            def _():
                out_v[k] = dot(own[0], own[f]).astype(out_v.dtype)

            @pl.when(f < 0)
            def _():
                out_v[k] = jnp.zeros(out_v.shape[1:], out_v.dtype)

            out_copy(k).start()

    @pl.loop(0, WIDTH)
    def _(k):
        _, active = job(k)

        @pl.when(active)
        def _():
            out_copy(k).wait()


def finish(table, own, right, slot, out_v, t):
    f = table[1, slot]

    @pl.when(f >= 0)
    def _():
        out_v[t] = (dot(own[0], own[f]) + dot(own[1], right())).astype(out_v.dtype)

    @pl.when(f < 0)
    def _():
        out_v[t] = dot(own[1], right()).astype(out_v.dtype)


def chunk_kernel(first_slot, jobs, table, own, chunk, band, out, out_v, sems):
    rows = own.shape[1]

    def out_copy(t):
        return pltpu.make_async_copy(out_v.at[t], out.at[0, table[0, first_slot + t]], sems.at[t])

    @pl.loop(0, jobs)
    def _(t):
        @pl.when(table[0, first_slot + t] >= 0)
        def _():
            finish(table, own, lambda: chunk[pl.ds(pl.multiple_of(t * rows, rows), rows)], first_slot + t, out_v, t)
            out_copy(t).start()

    @pl.loop(0, jobs)
    def _(t):
        @pl.when(table[0, first_slot + t] >= 0)
        def _():
            out_copy(t).wait()


def rest_kernel(last_device, first_slot, jobs, table, own, chunk, direct, detour, band, out, rest, out_v, sems):
    here = table[1, LAST + 1]

    @pl.when(here == last_device)
    def _():
        rest[...] = detour[...]

    @pl.when(here != last_device)
    def _():
        rest[...] = direct[...]

    chunk_kernel(first_slot, jobs, table, own, chunk, band, out, out_v, sems)


def base_kernel(first_slot, jobs, table, own, chunk, band, out, base, out_v, sems):
    f = table[1, LAST]

    @pl.when(f >= 0)
    def _():
        base[...] = dot(own[0], own[f])

    @pl.when(f < 0)
    def _():
        base[...] = jnp.zeros(base.shape, base.dtype)

    chunk_kernel(first_slot, jobs, table, own, chunk, band, out, out_v, sems)


def late_kernel(last_device, table, own, chunk, rest, direct, detour, near, base, band, out, low, left_v, out_v, sems):
    rows, half = left_v.shape
    fold = low.shape[0]
    k, k_last = table[0, LAST - 1], table[0, LAST]
    even = table[0, LAST + 1] == 0

    def tile(j):
        return pltpu.make_async_copy(out_v.at[j], out.at[0, table[0, LAST - 1 + j]], sems.at[j])

    @pl.when(k >= 0)
    def _():
        finish(table, own, lambda: chunk[:rows], LAST - 1, out_v, 0)
        tile(0).start()

    @pl.when((k_last >= 0) & jnp.logical_not(even))
    def _():
        low[: fold - DETOUR] = chunk[rows:]
        low[fold - DETOUR : fold - BLOCKS[1]] = rest[...]
        here = table[1, LAST + 1]
        around = (here == last_device) | (here == 3)

        @pl.when(around)
        def _():
            low[fold - BLOCKS[1] :] = detour[...]

        @pl.when(jnp.logical_not(around))
        def _():
            low[fold - BLOCKS[1] :] = direct[...]

        left = dot(own[1, :, :fold], low[:, :half]) + dot(own[1, :, fold:], low[:, half:])
        left_v[...] = (base[:, :half] + left).astype(left_v.dtype)
        left_copy = pltpu.make_async_copy(left_v, out.at[0, k_last, :, pl.ds(0, half)], sems.at[2])
        left_copy.start()
        left_copy.wait()

    @pl.when((k_last >= 0) & even)
    def _():
        out_v[1] = (base[...] + dot(own[1], near[...])).astype(out_v.dtype)
        tile(1).start()
        tile(1).wait()

    @pl.when(k >= 0)
    def _():
        tile(0).wait()


def last_kernel(place, own, chunk, base, band, out, out_v, sems):
    k = jnp.max(place[...])
    rows, half = chunk.shape
    blocks = sems.shape[0]

    def copy(j):
        block = pl.ds(j * (rows // blocks), rows // blocks)
        return pltpu.make_async_copy(out_v.at[block], out.at[0, k, block, pl.ds(half, half)], sems.at[j])

    for j in range(blocks):
        block = pl.ds(j * (rows // blocks), rows // blocks)
        out_v[block] = (base[block, half:] + dot(own[1, block], chunk[...])).astype(out_v.dtype)

        @pl.when(k >= 0)
        def _():
            copy(j).start()

    @pl.when(k >= 0)
    def _():
        for j in range(blocks):
            copy(j).wait()


def pack_kernel(pieces, noted, *refs):
    cols, counts, own, _ = refs[:4]
    parts, sem = refs[4:-1], refs[-1]
    copies = []
    for of_part, part in zip(pieces, parts):
        for slot, row, rows, lane, lanes, to_row, to_lane in of_part:
            copies.append(
                pltpu.make_async_copy(
                    own.at[slot, pl.ds(row, rows), pl.ds(lane, lanes)],
                    part.at[pl.ds(to_row, rows), pl.ds(to_lane, lanes)],
                    sem.at[len(copies)],
                )
            )
    for copy in copies:
        copy.start()
    if noted:
        size, lanes = parts[0].shape
        lane = lax.broadcasted_iota(jnp.int32, (META_ROWS, lanes), 1)
        note = jnp.zeros((META_ROWS, lanes), jnp.int32)
        slots = cols.shape[1]
        for s in range(slots):
            note = jnp.where(lane == s, cols[0, s], note)
        note = jnp.where(lane == slots, counts[0], note)
        parts[0][pl.ds(size - META_ROWS, META_ROWS)] = note.astype(jnp.float32).astype(parts[0].dtype)
    for copy in copies:
        copy.wait()


def params():
    return pltpu.CompilerParams(vmem_limit_bytes=20 * 2**20)


def pack(pieces, noted, cols, counts, own, after):
    shapes = []
    for of_part in pieces:
        shapes.append((max(p[5] + p[2] for p in of_part), max(p[6] + p[4] for p in of_part)))
    if noted:
        shapes[0] = (shapes[0][0] + META_ROWS, shapes[0][1])
    return pl.pallas_call(
        functools.partial(pack_kernel, pieces, noted),
        out_shape=[jax.ShapeDtypeStruct(shape, own.dtype) for shape in shapes],
        in_specs=[SMEM] * 2 + [HBM, ANY],
        out_specs=[VMEM] * len(shapes),
        scratch_shapes=[pltpu.SemaphoreType.DMA((sum(map(len, pieces)),))],
        compiler_params=params(),
        cost_estimate=pl.CostEstimate(flops=0, bytes_accessed=8 * sum(a * b for a, b in shapes), transcendentals=0),
    )(cols, counts, pltpu.with_memory_space_constraint(own, pltpu.HBM), after)


def call(kernel, weight, operands, spaces, scratch, extra=(), extra_specs=(), own=None):
    b = own.shape[1:]
    band = jax.ShapeDtypeStruct((1, WIDTH) + b, own.dtype)
    last = len(operands) - 1
    alone = operands[last].shape != band.shape
    return pl.pallas_call(
        kernel,
        out_shape=[band, *extra],
        in_specs=spaces,
        out_specs=[ANY, *extra_specs],
        input_output_aliases={} if alone else {last: 0},
        scratch_shapes=scratch,
        compiler_params=params(),
        cost_estimate=pl.CostEstimate(
            flops=weight * 4 * b[0] * b[0] * b[1], bytes_accessed=weight * b[0] * b[1] * 2, transcendentals=0
        ),
    )(*operands)


def per_device(tile_values, tile_cols, tile_counts):
    total = lax.axis_size("wide")
    own = tile_values
    slots, rows, lanes = own.shape
    pairs = [(i, (i - 1) % total) for i in range(total)]
    send = lambda value, some=pairs: lax.ppermute(value, "wide", some)
    tile = lambda *n: pltpu.VMEM(n + (rows, lanes), own.dtype)
    sems = lambda *n: pltpu.SemaphoreType.DMA(n)

    half, fold = lanes // 2, rows // 2
    whole = lambda a, b: tuple((s, 0, rows, 0, lanes, (s - a) * rows, 0) for s in range(a, b))
    folded = lambda a, b, at: tuple((LAST, j * fold + a, b - a, 0, half, at, j * half) for j in range(2))

    first = own[0]
    head = send(first)
    cut = fold - BLOCKS[1]
    one, end_a = pack([whole(1, 2), folded(fold - DETOUR, cut, 0)], True, tile_cols, tile_counts, own, first)
    two, local = pack([whole(*MIDDLE[1]), whole(0, slots)], False, tile_cols, tile_counts, own, one)
    three, end_b = pack([whole(*MIDDLE[2]), folded(cut, fold, 0)], False, tile_cols, tile_counts, own, head)
    chunks = [send(part) for part in (one, two, three)]
    four, five, seven = pack(
        [whole(LAST - 1, LAST) + folded(0, fold - DETOUR, rows), ((LAST, 0, rows, half, half, 0, 0),), whole(LAST, LAST + 1)],
        False, tile_cols, tile_counts, own, chunks[0],
    )
    late = send(four)
    groups = lax.axis_size("groups")
    across = [(g * total, (g ^ 1 if groups % 2 == 0 else g) * total) for g in range(groups)]
    both = lambda value, some: lax.ppermute(value, ("groups", "wide"), some)
    straight = [(g * total + i, g * total + j) for g in range(groups) for i, j in pairs[2::2]]
    shift = lambda some: [(g + i, h + j) for g, h in across for i, j in some]
    direct_a = both(end_a, straight + shift([(0, 2)]))
    direct_b = both(end_b, [p for p in straight if p[0] % total != 4] + shift([(0, 2), (4, 6)]))
    detour_a = both(direct_a, shift([(2, total - 1)]))
    detour_b = both(direct_b, shift([(2, total - 1), (6, 3)]))
    near = send(seven, pairs[1::2])
    far = send(five, pairs[0::2])
    local = local.reshape(own.shape)

    (band,) = call(head_kernel, 12, (local, head), [VMEM] * 2, [tile(), sems()], own=own)
    got = chunks[0][rows, : slots + 1].astype(jnp.int32)
    band, table, place = call(
        functools.partial(early_kernel, total), 3 * WIDTH,
        (tile_cols, tile_counts, got[None, :slots], got[slots:], local, band),
        [SMEM] * 4 + [VMEM, ANY], [tile(WIDTH), sems(WIDTH)],
        [jax.ShapeDtypeStruct((2, slots + 1), jnp.int32), jax.ShapeDtypeStruct((8, 128), jnp.int32)], [SMEM, VMEM], own=own,
    )
    a, b = MIDDLE[0]
    band, base = call(
        functools.partial(base_kernel, a, b - a), b - a,
        (table, local, chunks[0], band), [SMEM] + [VMEM] * 2 + [ANY], [tile(b - a), sems(b - a)],
        [jax.ShapeDtypeStruct((rows, lanes), jnp.float32)], [VMEM], own=own,
    )
    a, b = MIDDLE[1]
    band, rest = call(
        functools.partial(rest_kernel, total - 1, a, b - a), b - a,
        (table, local, chunks[1], direct_a, detour_a, band), [SMEM] + [VMEM] * 4 + [ANY], [tile(b - a), sems(b - a)],
        [jax.ShapeDtypeStruct((BLOCKS[0], lanes), own.dtype)], [VMEM], own=own,
    )
    a, b = MIDDLE[2]
    (band,) = call(
        functools.partial(chunk_kernel, a, b - a), b - a,
        (table, local, chunks[2], band), [SMEM] + [VMEM] * 2 + [ANY], [tile(b - a), sems(b - a)], own=own,
    )
    side = pltpu.VMEM((rows, half), own.dtype)
    (band,) = call(
        functools.partial(late_kernel, total - 1), 2,
        (table, local, late, rest, direct_b, detour_b, near, base, band), [SMEM] + [VMEM] * 7 + [ANY],
        [pltpu.VMEM((fold, lanes), own.dtype), side, tile(2), sems(3)], own=own,
    )
    (band,) = call(
        last_kernel, 1, (place, local, far, base, band), [VMEM] * 4 + [ANY], [side, sems(4)], own=own,
    )
    return band


def solution(mesh):
    placed = (P(("groups", "wide"), None, None), P(("groups", "wide"), None), P(("groups", "wide")))
    return jax.shard_map(
        per_device,
        mesh=mesh,
        in_specs=placed,
        out_specs=P(("groups", "wide"), None, None, None),
        check_vma=False,
    )
```
